256 devices in a mesh: seq: 32 (over y, x, core), dp: 8 (over z).
Axes of the slice: x: 4, y: 4, z: 8, core: 2. Of those that a mesh axis runs over, the one named last changes fastest.
Arguments:
- queries: bfloat16 [16384, 4096], P('seq', 'dp'), may hold values from -6 to 6
- keys: bfloat16 [16384, 4096], P('seq', 'dp'), may hold values from -6 to 6
- values: bfloat16 [16384, 4096], P('seq', 'dp'), may hold values from -102 to 102
- out_grad: bfloat16 [16384, 4096], P('seq'), may hold values from -6 to 6
- gain: bfloat16 [32, 128], P('dp', 'seq'), may hold values from 0.099609375 to 1.8984375
- out_weight: bfloat16 [4096, 4096], P('dp', 'seq'), may hold values from -0.09375 to 0.09375
Outputs:
- query_grad: bfloat16 [16384, 4096], P('seq', 'dp')
- key_grad: bfloat16 [16384, 4096], P('seq', 'dp')
- value_grad: bfloat16 [16384, 4096], P('seq', 'dp')
- weight_grad: float32 [4096, 4096], P('dp', 'seq')
- gain_grad: float32 [32, 128], P('dp', 'seq')
The draws below stay inside these ranges and needn't reach their ends.
All inputs are finite; a program needn't handle non-finite values.
Results may differ from the reference program's by a relative error of at most 0.006.
Values may be sent and summed in bfloat16 or wider, within the bound.
A program may use at most 128 MiB of HBM per device.

```python
import math
import jax
import jax.numpy as jnp
from jax import lax

HEADS = 32
HD = 128
BLK = 512
TOK_DEV = 512
D = 4096
SEQLEN = 16384
N_SEQ = 32


def draw_values(key, part):
    key = jax.random.fold_in(key, 11)
    first, second = jax.random.split(key, 2)
    column = jnp.exp(math.log(10.0) * jax.random.uniform(first, (D,), jnp.float32))
    head = (jnp.arange(D, dtype=jnp.int32) // HD).astype(jnp.float32)
    ramp = jnp.exp(math.log(3.0) * head / max(HEADS - 1, 1))
    base = jnp.clip(jax.random.normal(second, (SEQLEN, D), jnp.float32), -4.0, 4.0)
    return (0.5 * base * column * ramp).astype(jnp.bfloat16)


def strengthened(drawn, own_key, source, target, blocks, factor):
    owner, partner = [(jnp.arange(drawn.shape[axis_at]) // (drawn.shape[axis_at] // blocks)).reshape([-1 if axis == axis_at else 1 for axis in range(drawn.ndim)]) for axis_at in (source, target)]
    chosen = jax.random.permutation(own_key, blocks)[partner]
    strong = (owner == chosen) | (owner == (partner + blocks // 2) % blocks)
    return jnp.where(strong, factor * drawn, drawn)


def level_of(rng, shape, cuts, low, largest):
    factor_of, own = 1.0, jax.random.fold_in(rng, 6)
    for position, blocks in cuts:
        steps = jnp.exp(jax.random.uniform(jax.random.fold_in(own, position), (blocks,), jnp.float32, low / len(cuts), largest / len(cuts)))
        factor_of = factor_of * jnp.repeat(steps, shape[position] // blocks).reshape([-1 if axis == position else 1 for axis in range(len(shape))])
    return factor_of


def normal_values(stream_key, extent, deviation, reach, cuts=(), kind=jnp.bfloat16):
    loudness = level_of(stream_key, extent, cuts, -0.22, 0.18) if cuts else 1.0
    values = jax.random.normal(stream_key, extent, jnp.float32) * deviation * loudness
    return jnp.minimum(jnp.maximum(values, -reach), reach).astype(kind)


def gaussian_with(key, extent, spread, bound, cuts, heavy, held_as=jnp.bfloat16):
    values = spread * jax.random.normal(key, extent, jnp.float32)
    if cuts:
        values = values * level_of(key, extent, cuts, -0.22, 0.18)
    return jnp.clip(strengthened(values, jax.random.fold_in(key, 3), *heavy), -bound, bound).astype(held_as)


def setup_inputs(seed: int = 0) -> dict:
    arg_keys = jax.random.split(jax.random.key(seed), 7)
    return {
        "queries": normal_values(arg_keys[0], (SEQLEN, D), 1.0, 6.0, ((0, 32), (1, 8))),
        "keys": normal_values(arg_keys[1], (SEQLEN, D), 1.0, 6.0, ((0, 32), (1, 8))),
        "values": draw_values(jax.random.fold_in(arg_keys[6], 71), 0),
        "out_grad": gaussian_with(arg_keys[3], (SEQLEN, D), 1.0, 6.0, ((0, 32),), (0, 1, 32, 2.75)),
        "gain": jnp.clip(1.0 + 0.18 * jax.random.normal(arg_keys[4], (HEADS, HD), jnp.float32), 0.099609375, 1.8984375).astype(jnp.bfloat16),
        "out_weight": normal_values(arg_keys[5], (D, D), D ** -0.5, 0.09375, ((0, 8), (1, 32))),
    }


EPSILON = 1e-06

def causal_mask(size):
    rows = lax.broadcasted_iota(jnp.int32, (size, size), 0)
    cols = lax.broadcasted_iota(jnp.int32, (size, size), 1)
    return (cols <= rows).astype(jnp.float32)

def block_scores(query_block, key_block, lower):
    raw = jnp.einsum('thi,uhi->htu', query_block.astype(jnp.float32), key_block.astype(jnp.float32))
    return (raw * lower).astype(jnp.bfloat16)

def reference(queries, keys, values, out_grad, gain, out_weight):
    total = queries.shape[0]
    count = total // BLK
    lower = causal_mask(BLK)

    def split(array):
        return array.reshape(count, BLK, HEADS, HD)
    query_blocks = split(queries)
    key_blocks = split(keys)
    value_blocks = split(values)

    def forward(state, block):
        query_block, key_block, value_block = block
        scores = block_scores(query_block, key_block, lower)
        state_in = state.astype(jnp.bfloat16)
        query_f = query_block.astype(jnp.float32)
        key_f = key_block.astype(jnp.float32)
        value_f = value_block.astype(jnp.float32)
        result = jnp.einsum('htu,uhj->thj', scores.astype(jnp.float32), value_f)
        result = result + jnp.einsum('thi,hij->thj', query_f, state_in.astype(jnp.float32))
        return (state + jnp.einsum('thi,thj->hij', key_f, value_f), (result, state_in))
    zero_state = jnp.zeros((HEADS, HD, HD), jnp.float32)
    _, (attended, states_in) = lax.scan(forward, zero_state, (query_blocks, key_blocks, value_blocks))
    attended = attended.reshape(total, D)
    gain_flat = gain.reshape(D).astype(jnp.float32)
    inv_rms = lax.rsqrt(lax.optimization_barrier(jnp.sum(attended * attended, axis=1)) / D + EPSILON)
    normed = (attended * inv_rms[:, None] * gain_flat).astype(jnp.bfloat16)
    upstream = jnp.dot(out_grad, out_weight.T, preferred_element_type=jnp.float32)
    weighted = upstream * gain_flat
    inner = lax.optimization_barrier(jnp.sum(weighted * attended, axis=1))
    p_grad = (inv_rms[:, None] * weighted - attended * (inv_rms ** 3 * inner / D)[:, None]).astype(jnp.bfloat16)
    gain_terms = upstream * attended * inv_rms[:, None]

    def partial_sums(carry, pieces):
        normed_part, grad_part, gain_part = pieces
        term = jnp.dot(normed_part.T, grad_part, preferred_element_type=jnp.float32)
        gain_term = lax.optimization_barrier(jnp.sum(gain_part, axis=0))
        return ((carry[0] + term, carry[1] + gain_term), None)
    start = (jnp.zeros((D, D), jnp.float32), jnp.zeros((D,), jnp.float32))
    (weight_grad, gain_flat_grad), _ = lax.scan(partial_sums, start, (normed.reshape(N_SEQ, TOK_DEV, D), out_grad.reshape(N_SEQ, TOK_DEV, D), gain_terms.reshape(N_SEQ, TOK_DEV, D)))
    gain_grad = gain_flat_grad.reshape(HEADS, HD)
    grad_blocks = split(p_grad)

    def backward(later, block):
        query_block, key_block, value_block, grad_block, state_in = block
        scores = block_scores(query_block, key_block, lower)
        later_in = later.astype(jnp.bfloat16)
        query_f = query_block.astype(jnp.float32)
        key_f = key_block.astype(jnp.float32)
        value_f = value_block.astype(jnp.float32)
        grad_f = grad_block.astype(jnp.float32)
        back = jnp.einsum('thj,uhj->htu', grad_f, value_f)
        back = (back * lower).astype(jnp.bfloat16).astype(jnp.float32)
        state_f = state_in.astype(jnp.float32)
        later_f = later_in.astype(jnp.float32)
        dquery = jnp.einsum('htu,uhi->thi', back, key_f) + jnp.einsum('thj,hij->thi', grad_f, state_f)
        dkey = jnp.einsum('htu,thi->uhi', back, query_f) + jnp.einsum('uhj,hij->uhi', value_f, later_f)
        dvalue = jnp.einsum('htu,thj->uhj', scores.astype(jnp.float32), grad_f) + jnp.einsum('uhi,hij->uhj', key_f, later_f)
        update = jnp.einsum('thi,thj->hij', query_f, grad_f)
        return (later + update, (dquery.astype(jnp.bfloat16), dkey.astype(jnp.bfloat16), dvalue.astype(jnp.bfloat16)))
    _, (query_grad, key_grad, value_grad) = lax.scan(backward, zero_state, (query_blocks, key_blocks, value_blocks, grad_blocks, states_in), reverse=True)
    return (query_grad.reshape(total, D), key_grad.reshape(total, D), value_grad.reshape(total, D), weight_grad, gain_grad)
```

```python
import jax
import jax.numpy as jnp
from jax import lax
from jax.experimental import pallas as pl
from jax.experimental.pallas import tpu as pltpu
from jax.sharding import PartitionSpec as P

HD = 128
TOK = 512
WID = 512
NH = 4
D = 4096
EPSILON = 1e-06
HALF = 256
BF = jnp.bfloat16
F32 = jnp.float32
MESH = pl.DeviceIdType.MESH
STEPS = (0, 3, 1, 2)
ORDER = (2, 1, 3, 0)


def nt(a, b):
    return lax.dot_general(a, b, (((1,), (1,)), ((), ())), preferred_element_type=F32)


def tn(a, b):
    return lax.dot_general(a, b, (((0,), (0,)), ((), ())), preferred_element_type=F32)


def nn(a, b):
    return jnp.dot(a, b, preferred_element_type=F32)


def layer_kernel(
    q_hbm, k_hbm, v_hbm, og_hbm, gain_ref, w_hbm,
    dq_hbm, dk_hbm, dv_hbm, wg_hbm, gg_ref,
    q, k, v, og, wall, scores_t, q_t, att, up, p, n_t, dkp, dvp, dq_o, dk_o, dv_o, wg_o,
    kvs, s0s, s0r, s1s, s1r, s2s, s2r, fin, st, zb, gflat, col,
    sib_out, sib_in, part, ra, pb_buf, rb,
    load_sem, out_sem, ag_send, ag_recv, ag_sib, sc_send, sc_recv, z_send, z_recv,
    rs_send, rs_recv, rsb_recv, pair_send, pair_recv,
):
    s = lax.axis_index("seq")
    z = lax.axis_index("dp")
    y, x, c = s // 8, (s // 2) % 4, s % 2
    o = 1 - c
    pa, pb = x + c * (y - x), y + c * (x - y)

    def chip(da, db):
        a, b = (pa + da) % 4, (pb + db) % 4
        return a * (1 + 3 * c) + b * (4 - 3 * c)

    def chip_o(da, db):
        a, b = (pb + da) % 4, (pa + db) % 4
        return a * (1 + 3 * o) + b * (4 - 3 * o)

    def dev(da, db):
        return (2 * chip(da, db) + c, z)

    sib = (s + 1 - 2 * c, z)

    loads = [
        pltpu.make_async_copy(src, dst, load_sem.at[i])
        for i, (src, dst) in enumerate(
            [(k_hbm, k), (v_hbm, v), (w_hbm, wall.at[s]), (q_hbm, q), (og_hbm, og)]
        )
    ]
    for load in loads:
        load.start()

    barrier = pltpu.get_barrier_semaphore()
    partners = [dev(i, 0) for i in (1, 2, 3)] + [dev(0, i) for i in (1, 2, 3)] + [sib]
    partners += [(s, (z + i) % 8) for i in range(1, 8)]
    for d in partners:
        pl.semaphore_signal(barrier, inc=1, device_id=d, device_id_type=MESH)

    def send(src, dst, ssem, rsem, d):
        pltpu.make_async_remote_copy(
            src_ref=src, dst_ref=dst, send_sem=ssem, recv_sem=rsem,
            device_id=d, device_id_type=MESH,
        ).start()

    def await_(ref, sem):
        pltpu.make_async_copy(ref, ref, sem).wait()

    def head(h):
        return pl.ds(pl.multiple_of(h * HD, HD), HD)

    def rows(h, n=HD):
        return pl.ds(pl.multiple_of(h * n, n), n)

    lane = lax.broadcasted_iota(jnp.int32, (HD, HD), 1)
    subl = lax.broadcasted_iota(jnp.int32, (HD, HD), 0)
    eye = lane == subl

    def to_rows(column):
        return jnp.sum(jnp.where(eye, column, 0.0), axis=0, keepdims=True)

    def to_column(row):
        return jnp.sum(jnp.where(eye, row, 0.0), axis=1, keepdims=True)

    def two(rows4):
        high = rows4.astype(BF).astype(F32)
        return jnp.concatenate([high, rows4 - high, jnp.zeros((8, HD), F32)], axis=0)

    def one(rows16):
        return rows16[:NH] + rows16[NH:2 * NH]

    def before(i, j, backward):
        return (i > j) if backward else (i < j)

    own_half = rows(c, HALF)

    def scan_start(n, extra):
        s0s[n, 0:HALF, :] = kvs[n, rows(o, HALF), :]
        s0s[n, HALF:, :] = extra
        send(s0s.at[n], s0r.at[n], sc_send.at[n, 0], sc_recv.at[n, 0], sib)

    def scan_ring_a(n, extra):
        await_(s0r.at[n], sc_recv.at[n, 0])
        s1s[n, 0:HALF, :] = (kvs[n, own_half, :] + s0r[n, 0:HALF, :]).astype(BF)
        s1s[n, HALF:, :] = two(one(extra + s0r[n, HALF:, :])).astype(BF)
        for i in (1, 2, 3):
            send(s1s.at[n], s1r.at[n, i - 1], sc_send.at[n, 1], sc_recv.at[n, i], dev(i, 0))

    def scan_ring_b(n, backward):
        for i in (1, 2, 3):
            await_(s1r.at[n, i - 1], sc_recv.at[n, i])
        mine = s1s[n].astype(F32)
        lower, total = jnp.zeros_like(mine), mine
        for i in (1, 2, 3):
            got = s1r[n, i - 1].astype(F32)
            flag = before((pa - i + 4) % 4, pa, backward)
            lower = lower + jnp.where(flag, got, 0.0)
            total = total + got
        first = c == 0
        low = jnp.where(first, total, lower)
        high = jnp.where(first, total, lower + mine)
        s2s[n, 0, 0:HALF, :] = low[:HALF].astype(BF)
        s2s[n, 1, 0:HALF, :] = high[:HALF].astype(BF)
        s2s[n, 0, HALF:, :] = two(one(total[HALF:])).astype(BF)
        s2s[n, 1, HALF:, :] = two(one(total[HALF:])).astype(BF)
        for i in (1, 2, 3):
            pick = before(pb, (pb + i) % 4, backward).astype(jnp.int32)
            send(s2s.at[n, pick], s2r.at[n, i - 1], sc_send.at[n, 2], sc_recv.at[n, 3 + i], dev(0, i))
        return lower[:HALF], total[HALF:]

    def scan_last(n, backward, lower, extra):
        for i in (1, 2, 3):
            await_(s2r.at[n, i - 1], sc_recv.at[n, 3 + i])
        for i in (1, 2, 3):
            got = s2r[n, i - 1].astype(F32)
            flag = jnp.logical_or(c == 1, before((pb - i + 4) % 4, pb, backward))
            lower = lower + jnp.where(flag, got[:HALF], 0.0)
            extra = extra + got[HALF:]
        far = 0 if backward else 1
        fin[n] = (lower + jnp.where(o == far, kvs[n, own_half, :], 0.0)).astype(BF)
        send(fin.at[n], st.at[n, own_half], sc_send.at[n, 3], sc_recv.at[n, 7], sib)
        st[n, own_half, :] = (lower + jnp.where(c == far, s0r[n, 0:HALF, :], 0.0)).astype(BF)
        return one(extra)

    def scan_end(n):
        await_(fin.at[n], sc_recv.at[n, 7])

    def scan_drain(n):
        await_(s0s.at[n], sc_send.at[n, 0])
        await_(s1r.at[n], sc_send.at[n, 1])
        await_(s2r.at[n], sc_send.at[n, 2])
        await_(fin.at[n], sc_send.at[n, 3])

    def z_start(n):
        for i in range(1, 8):
            slot = zb.at[n, z]
            send(slot, slot, z_send.at[n], z_recv.at[n, i - 1], (s, (z + i) % 8))

    def z_end(n):
        for i in range(1, 8):
            await_(zb.at[n, z], z_recv.at[n, i - 1])
        total = zb[n, 0]
        for i in range(1, 8):
            total = total + zb[n, i]
        return total

    def z_drain(n):
        await_(zb.at[n, pl.ds(0, 7)], z_send.at[n])

    low_rows, high_rows = pl.ds(0, HALF), pl.ds(HALF, HALF)

    def piece(da, db):
        return wall.at[2 * chip(da, db) + c]

    def piece_o(da, db):
        return wall.at[2 * chip_o(da, db) + o]

    def ag_full(ref, event, d):
        send(ref, ref, ag_send.at[0], ag_recv.at[event], d)

    def ag_pair(ref, i, j):
        send(ref, ref, ag_send.at[0], ag_sib.at[4 * i + j], sib)

    def ag_own():
        ref = piece(0, 0)
        ag_full(ref, 0, dev(1, 0))
        ag_full(ref, 1, dev(3, 0))
        ag_full(ref, 4, dev(0, 1))
        ag_full(ref, 5, dev(0, 3))
        ag_pair(ref, 0, 0)

    def ag_a(i):
        da = STEPS[i]
        ref = piece(da, 0)
        if i == 3:
            await_(ref.at[low_rows], ag_recv.at[2])
            await_(ref.at[high_rows], ag_recv.at[3])
        else:
            await_(ref, ag_recv.at[i - 1])
            part_rows = low_rows if i == 1 else high_rows
            half = ref.at[part_rows]
            send(half, half, ag_send.at[0], ag_recv.at[1 + i], dev(1 if i == 1 else 3, 0))
        ag_full(ref, 4 + 4 * i, dev(0, 1))
        ag_full(ref, 5 + 4 * i, dev(0, 3))
        ag_pair(ref, i, 0)

    def ag_b(i):
        da = STEPS[i]
        for j in (1, 2):
            ref = piece(da, STEPS[j])
            await_(ref, ag_recv.at[4 + 4 * i + j - 1])
            half = ref.at[low_rows if j == 1 else high_rows]
            send(half, half, ag_send.at[0], ag_recv.at[5 + 4 * i + j], dev(0, 1 if j == 1 else 3))
            ag_pair(ref, i, j)

    def ag_b_far(i):
        ref = piece(STEPS[i], 2)
        await_(ref.at[low_rows], ag_recv.at[6 + 4 * i])
        await_(ref.at[high_rows], ag_recv.at[7 + 4 * i])
        ag_pair(ref, i, 3)

    def ag_pair_end(j):
        for i in range(4):
            await_(piece_o(STEPS[i], STEPS[j]), ag_sib.at[4 * i + j])

    def ag_drain():
        await_(wall.at[pl.ds(0, 31)], ag_send.at[0])

    def upstream(j):
        mine = [2 * chip(STEPS[i], STEPS[j]) + c for i in range(4)]
        mine += [2 * chip_o(STEPS[i], STEPS[j]) + o for i in range(4)]
        grad = jnp.concatenate([og[:, head(m)] for m in mine], axis=1)
        for n in (0, HALF):
            weight = jnp.concatenate([wall[m, n:n + HALF, :] for m in mine], axis=1)
            term = nt(grad, weight)
            up[:, n:n + HALF] = term if j == 0 else up[:, n:n + HALF] + term

    def ordered(j):
        return jnp.where(j == 0, 2, jnp.where(j == 3, 0, jnp.where(j == 1, 1, 3)))

    def rs_pair_out():
        def pair(i, _):
            jb, h = i // 2, i % 2
            db = ordered(jb)
            m0 = 2 * chip_o(ordered(2 * h), db) + o
            m1 = 2 * chip_o(ordered(2 * h + 1), db) + o
            term = nn(n_t[...], jnp.concatenate([og[:, head(m0)], og[:, head(m1)]], axis=1))
            sib_out[2 * i] = term[:, :HD].astype(BF)
            sib_out[2 * i + 1] = term[:, HD:].astype(BF)
            slot = pl.ds(2 * i, 2)
            send(sib_out.at[slot], sib_in.at[slot], pair_send.at[0], pair_recv.at[i], sib)
            return _

        lax.fori_loop(0, 8, pair, 0)

    def rs_send_to(src, dst, rsem, d):
        send(src, dst, rs_send.at[0], rsem, d)

    def rs_own():
        def group(jb, _):
            db = ordered(jb)
            for h in (0, 1):
                m0 = 2 * chip(ORDER[2 * h], db) + c
                m1 = 2 * chip(ORDER[2 * h + 1], db) + c
                term = nn(n_t[...], jnp.concatenate([og[:, head(m0)], og[:, head(m1)]], axis=1))
                i = 2 * jb + h
                await_(sib_in.at[pl.ds(2 * i, 2)], pair_recv.at[i])
                part[2 * i] = (term[:, :HD] + sib_in[2 * i].astype(F32)).astype(BF)
                part[2 * i + 1] = (term[:, HD:] + sib_in[2 * i + 1].astype(F32)).astype(BF)
                if h == 0:
                    far, near = part.at[2 * i], part.at[2 * i + 1]
                    rs_send_to(far.at[low_rows], ra.at[jb, 0], rs_recv.at[jb, 0], dev(1, 0))
                    rs_send_to(far.at[high_rows], ra.at[jb, 1], rs_recv.at[jb, 1], dev(3, 0))
                    rs_send_to(near.at[high_rows], ra.at[jb, 2], rs_recv.at[jb, 2], dev(1, 0))
                else:
                    near = part.at[2 * i]
                    rs_send_to(near.at[low_rows], ra.at[jb, 4], rs_recv.at[jb, 4], dev(3, 0))
            return _

        lax.fori_loop(0, 4, group, 0)

    def rs_a_mid(jb):
        await_(ra.at[jb, 0], rs_recv.at[jb, 0])
        m = 4 * jb + 1
        part[m, 0:HALF, :] = (part[m, 0:HALF, :].astype(F32) + ra[jb, 0].astype(F32)).astype(BF)
        rs_send_to(part.at[m, low_rows], ra.at[jb, 3], rs_recv.at[jb, 3], dev(1, 0))
        await_(ra.at[jb, 1], rs_recv.at[jb, 1])
        m = 4 * jb + 2
        part[m, HALF:, :] = (part[m, HALF:, :].astype(F32) + ra[jb, 1].astype(F32)).astype(BF)
        rs_send_to(part.at[m, high_rows], ra.at[jb, 5], rs_recv.at[jb, 5], dev(3, 0))

    def rs_a_end(jb):
        for i in (2, 3, 4, 5):
            await_(ra.at[jb, i], rs_recv.at[jb, i])
        m = 4 * jb + 3
        top = part[m, 0:HALF, :].astype(F32) + ra[jb, 3].astype(F32) + ra[jb, 4].astype(F32)
        low = part[m, HALF:, :].astype(F32) + ra[jb, 2].astype(F32) + ra[jb, 5].astype(F32)
        if jb == 3:
            wg_o[0:HALF, :] = top
            wg_o[HALF:, :] = low
            return
        pb_buf[jb, 0:HALF, :] = top.astype(BF)
        pb_buf[jb, HALF:, :] = low.astype(BF)
        ref = pb_buf.at[jb]
        if jb == 0:
            rs_send_to(ref.at[low_rows], rb.at[0], rsb_recv.at[0], dev(0, 1))
            rs_send_to(ref.at[high_rows], rb.at[1], rsb_recv.at[1], dev(0, 3))
        elif jb == 1:
            rs_send_to(ref.at[high_rows], rb.at[2], rsb_recv.at[2], dev(0, 1))
        else:
            rs_send_to(ref.at[low_rows], rb.at[4], rsb_recv.at[4], dev(0, 3))

    def rs_b_mid():
        await_(rb.at[0], rsb_recv.at[0])
        pb_buf[1, 0:HALF, :] = (pb_buf[1, 0:HALF, :].astype(F32) + rb[0].astype(F32)).astype(BF)
        rs_send_to(pb_buf.at[1, low_rows], rb.at[3], rsb_recv.at[3], dev(0, 1))
        await_(rb.at[1], rsb_recv.at[1])
        pb_buf[2, HALF:, :] = (pb_buf[2, HALF:, :].astype(F32) + rb[1].astype(F32)).astype(BF)
        rs_send_to(pb_buf.at[2, high_rows], rb.at[5], rsb_recv.at[5], dev(0, 3))

    def rs_b_end():
        for i in (2, 3, 4, 5):
            await_(rb.at[i], rsb_recv.at[i])
        wg_o[0:HALF, :] = wg_o[0:HALF, :] + rb[3].astype(F32) + rb[4].astype(F32)
        wg_o[HALF:, :] = wg_o[HALF:, :] + rb[2].astype(F32) + rb[5].astype(F32)

    def rs_drain():
        await_(sib_in.at[pl.ds(0, 15)], rs_send.at[0])
        await_(sib_out, pair_send.at[0])

    tri_r = lax.broadcasted_iota(jnp.int32, (HALF, HALF), 0)
    tri_u = lax.broadcasted_iota(jnp.int32, (HALF, HALF), 1)

    def lower_part(a, b):
        return jnp.where(tri_u <= tri_r, nt(a, b), 0.0).astype(BF)

    def upper_part(a, b):
        return jnp.where(tri_u >= tri_r, nt(a, b), 0.0).astype(BF)

    top, bot = slice(0, HALF), slice(HALF, TOK)

    def forward_head(h):
        l = head(h)
        q0, q1, k0, k1 = q[top, l], q[bot, l], k[top, l], k[bot, l]
        att[top, l] = nn(lower_part(q0, k0), v[top, l])
        both = jnp.concatenate([nt(q1, k0).astype(BF), lower_part(q1, k1)], axis=1)
        att[bot, l] = nn(both, v[:, l])
        scores_t[h, top, top] = upper_part(k0, q0)
        scores_t[h, top, bot] = nt(k0, q1).astype(BF)
        scores_t[h, bot, bot] = upper_part(k1, q1)

    def back_head(h):
        l = head(h)
        p0, p1, v0, v1 = p[top, l], p[bot, l], v[top, l], v[bot, l]
        state = st[0, rows(h), :]
        dq_o[top, l] = (nn(lower_part(p0, v0), k[top, l]) + nt(p0, state)).astype(BF)
        both = jnp.concatenate([nt(p1, v0).astype(BF), lower_part(p1, v1)], axis=1)
        dq_o[bot, l] = (nn(both, k[:, l]) + nt(p1, state)).astype(BF)
        both = jnp.concatenate([upper_part(v0, p0), nt(v0, p1).astype(BF)], axis=1)
        dkp[top, l] = nn(both, q[:, l])
        dkp[bot, l] = nn(upper_part(v1, p1), q[bot, l])
        dvp[top, l] = nn(scores_t[h, top, :], p[:, l])
        dvp[bot, l] = nn(scores_t[h, bot, bot], p1)

    def loop(lo, hi, f):
        def step(h, _):
            f(h)
            return _

        lax.fori_loop(lo, hi, step, 0)

    lane4 = lax.broadcasted_iota(jnp.int32, (NH, HD), 1)
    placed = jnp.zeros((NH, HD), F32)
    for j in range(4):
        placed = placed + jnp.where(lane4 == 4 * s + j, gain_ref[:, j:j + 1].astype(F32), 0.0)
    placed = jnp.concatenate([placed, jnp.zeros((16 - NH, HD), F32)], axis=0)
    loads[2].wait()
    pl.semaphore_wait(barrier, 14)
    ag_own()
    loads[0].wait()
    loads[1].wait()
    for h in range(NH):
        l = slice(h * HD, (h + 1) * HD)
        kvs[0, l, :] = tn(k[:, l], v[:, l])
    scan_start(0, placed)
    loads[3].wait()
    loop(0, 1, forward_head)
    scan_ring_a(0, placed)
    loop(1, 2, forward_head)
    ag_a(1)
    ag_a(2)
    loop(2, 3, forward_head)
    lower, extra = scan_ring_b(0, False)
    loop(3, 4, forward_head)
    ag_a(3)
    ag_b(0)
    gains = scan_last(0, False, lower, extra)
    for h in range(NH):
        gflat[0:1, h * HD:(h + 1) * HD] = gains[h:h + 1]
        q_t[h] = q[:, h * HD:(h + 1) * HD].T
    ag_b_far(0)
    scan_end(0)

    for h in range(NH):
        l = slice(h * HD, (h + 1) * HD)
        a = att[:, l] + nn(q[:, l], st[0, l, :])
        att[:, l] = a
        col[0] = a * a if h == 0 else col[0] + a * a
    for t in range(4):
        l = slice(t * 128, (t + 1) * 128)
        zb[0, z, t:t + 1, :] = to_rows(jnp.sum(col[0, l, :], axis=1, keepdims=True))
    z_start(0)
    ag_b(1)
    ag_b(2)
    loads[4].wait()
    ag_pair_end(0)
    upstream(0)
    ag_b_far(1)
    ag_b(3)
    ag_b_far(2)
    ag_pair_end(1)
    upstream(1)
    ag_b_far(3)
    ag_pair_end(2)
    upstream(2)
    ag_pair_end(3)
    upstream(3)

    def inner_block(t, _):
        r = rows(t, 128)
        total = jnp.zeros((HD, HD), F32)
        for h in range(NH):
            l = slice(h * HD, (h + 1) * HD)
            total = total + up[r, l] * gflat[0:1, l] * att[r, l]
        zb[1, z, pl.ds(t, 1), :] = to_rows(jnp.sum(total, axis=1, keepdims=True))
        return _

    lax.fori_loop(0, 4, inner_block, 0)
    z_start(1)
    squares = z_end(0)
    inv = lax.rsqrt(squares / D + EPSILON)
    for t in range(4):
        col[0, t * 128:(t + 1) * 128, :] = jnp.broadcast_to(to_column(inv[t:t + 1]), (HD, HD))

    def normed_block(t, _):
        r = rows(t, 128)
        for h in range(NH):
            l = slice(h * HD, (h + 1) * HD)
            normed = att[r, l] * col[0, r, :] * gflat[0:1, l]
            n_t[l, head(t)] = normed.astype(BF).T
        return _

    lax.fori_loop(0, 4, normed_block, 0)
    rs_pair_out()
    rs_own()
    inner = z_end(1)
    for t in range(4):
        pair = inv[t:t + 1] * inv[t:t + 1] * inv[t:t + 1] * inner[t:t + 1] / D
        col[1, t * 128:(t + 1) * 128, :] = jnp.broadcast_to(to_column(pair), (HD, HD))

    def grad_block(t, sums):
        r = rows(t, 128)
        out = []
        for h in range(NH):
            l = slice(h * HD, (h + 1) * HD)
            a, u, i = att[r, l], up[r, l], col[0, r, :]
            p[r, l] = (i * u * gflat[0:1, l] - a * col[1, r, :]).astype(BF)
            out.append(sums[h] + jnp.sum(u * a * i, axis=0, keepdims=True))
        return tuple(out)

    sums = lax.fori_loop(0, 4, grad_block, (jnp.zeros((1, HD), F32),) * NH)
    gain_part = jnp.concatenate(list(sums), axis=0)

    for h in range(NH):
        l = slice(h * HD, (h + 1) * HD)
        kvs[1, l, :] = nn(q_t[h], p[:, l])
    scan_start(1, two(gain_part))
    rs_a_mid(0)
    loop(0, 1, back_head)
    scan_ring_a(1, two(gain_part))
    rs_a_mid(1)
    rs_a_mid(2)
    loop(1, 2, back_head)
    lower, extra = scan_ring_b(1, True)
    rs_a_mid(3)
    rs_a_end(0)
    loop(2, 3, back_head)
    rs_a_end(1)
    gain_total = scan_last(1, True, lower, extra)
    loop(3, 4, back_head)
    dq_copy = pltpu.make_async_copy(dq_o, dq_hbm, out_sem.at[0])
    dq_copy.start()
    rs_a_end(2)
    rs_b_mid()
    for j in range(4):
        gg_ref[:, j:j + 1] = jnp.sum(
            jnp.where(lane4 == 4 * s + j, gain_total, 0.0), axis=1, keepdims=True
        )
    scan_end(1)
    for h in range(NH):
        l = slice(h * HD, (h + 1) * HD)
        dk_o[:, l] = (dkp[:, l] + nt(v[:, l], st[1, l, :])).astype(BF)
        dv_o[:, l] = (dvp[:, l] + nn(k[:, l], st[1, l, :])).astype(BF)
    dk_copy = pltpu.make_async_copy(dk_o, dk_hbm, out_sem.at[1])
    dv_copy = pltpu.make_async_copy(dv_o, dv_hbm, out_sem.at[2])
    dk_copy.start()
    dv_copy.start()
    ag_drain()
    scan_drain(0)
    z_drain(0)
    z_drain(1)
    rs_a_end(3)
    rs_b_end()
    wg_copy = pltpu.make_async_copy(wg_o, wg_hbm, out_sem.at[3])
    wg_copy.start()
    rs_drain()
    scan_drain(1)
    for copy in (dq_copy, dk_copy, dv_copy, wg_copy):
        copy.wait()


def copy_kernel(a, b, d, e, f, a_o, b_o, d_o, e_o, f_o, sem):
    copies = [
        pltpu.make_async_copy(src, dst, sem.at[i])
        for i, (src, dst) in enumerate([(a, a_o), (b, b_o), (d, d_o), (e, e_o), (f, f_o)])
    ]
    for copy in copies:
        copy.start()
    for copy in copies:
        copy.wait()


def body(queries, keys, values, out_grad, gain, out_weight):
    any_space = pl.BlockSpec(memory_space=pl.ANY)
    hbm = pl.BlockSpec(memory_space=pltpu.HBM)
    vmem = pl.BlockSpec(memory_space=pltpu.VMEM)
    sem = pltpu.SemaphoreType.DMA
    outs = (
        jax.ShapeDtypeStruct((TOK, WID), BF),
        jax.ShapeDtypeStruct((TOK, WID), BF),
        jax.ShapeDtypeStruct((TOK, WID), BF),
        jax.ShapeDtypeStruct((WID, HD), F32),
        jax.ShapeDtypeStruct((NH, 4), F32),
    )
    wide = lambda dt: pltpu.VMEM((TOK, WID), dt)
    results = pl.pallas_call(
        layer_kernel,
        out_shape=outs,
        in_specs=[hbm, hbm, hbm, hbm, vmem, hbm],
        out_specs=(any_space, any_space, any_space, any_space, vmem),
        scratch_shapes=[
            wide(BF), wide(BF), wide(BF),
            pltpu.VMEM((TOK, D), BF),
            pltpu.VMEM((32, WID, HD), BF),
            pltpu.VMEM((NH, TOK, TOK), BF),
            pltpu.VMEM((NH, HD, TOK), BF),
            wide(F32), wide(F32), wide(BF), wide(BF), wide(F32), wide(F32),
            wide(BF), wide(BF), wide(BF),
            pltpu.VMEM((WID, HD), F32),
            pltpu.VMEM((2, WID, HD), F32),
            pltpu.VMEM((2, HALF + 16, HD), F32),
            pltpu.VMEM((2, HALF + 16, HD), F32),
            pltpu.VMEM((2, HALF + 16, HD), BF),
            pltpu.VMEM((2, 3, HALF + 16, HD), BF),
            pltpu.VMEM((2, 2, HALF + 16, HD), BF),
            pltpu.VMEM((2, 3, HALF + 16, HD), BF),
            pltpu.VMEM((2, HALF, HD), BF),
            pltpu.VMEM((2, WID, HD), BF),
            pltpu.VMEM((2, 8, 4, HD), F32),
            pltpu.VMEM((1, WID), F32),
            pltpu.VMEM((2, TOK, HD), F32),
            pltpu.VMEM((16, WID, HD), BF),
            pltpu.VMEM((16, WID, HD), BF),
            pltpu.VMEM((16, WID, HD), BF),
            pltpu.VMEM((4, 6, HALF, HD), BF),
            pltpu.VMEM((3, WID, HD), BF),
            pltpu.VMEM((6, HALF, HD), BF),
            sem((5,)), sem((4,)), sem((1,)), sem((20,)), sem((16,)),
            sem((2, 4)), sem((2, 8)), sem((2,)), sem((2, 7)),
            sem((1,)), sem((4, 6)), sem((6,)), sem((1,)), sem((8,)),
        ],
        compiler_params=pltpu.CompilerParams(
            collective_id=0, has_side_effects=True, vmem_limit_bytes=52 * 2**20
        ),
        cost_estimate=pl.CostEstimate(
            flops=6_400_000_000, bytes_accessed=8_000_000, transcendentals=512
        ),
        name="layer",
    )(queries, keys, values, out_grad, gain, out_weight)
    return pl.pallas_call(
        copy_kernel,
        out_shape=outs,
        in_specs=[any_space] * 5,
        out_specs=(hbm,) * 5,
        scratch_shapes=[sem((5,))],
        compiler_params=pltpu.CompilerParams(vmem_limit_bytes=2**20),
        name="results",
    )(*results)


def solution(mesh):
    return jax.shard_map(
        body,
        mesh=mesh,
        in_specs=(
            P("seq", "dp"),
            P("seq", "dp"),
            P("seq", "dp"),
            P("seq", None),
            P("dp", "seq"),
            P("dp", "seq"),
        ),
        out_specs=(P("seq", "dp"), P("seq", "dp"), P("seq", "dp"), P("dp", "seq"), P("dp", "seq")),
        check_vma=False,
    )
```

```python
import jax
import jax.numpy as jnp
from jax import lax
from jax.experimental import pallas as pl
from jax.experimental.pallas import tpu as pltpu
from jax.sharding import PartitionSpec as P

HD = 128
TOK = 512
WID = 512
NH = 4
D = 4096
EPSILON = 1e-06
HALF = 256
BF = jnp.bfloat16
F32 = jnp.float32
MESH = pl.DeviceIdType.MESH
STEPS = (0, 3, 1, 2)
ORDER = (2, 1, 3, 0)


def nt(a, b):
    return lax.dot_general(a, b, (((1,), (1,)), ((), ())), preferred_element_type=F32)


def tn(a, b):
    return lax.dot_general(a, b, (((0,), (0,)), ((), ())), preferred_element_type=F32)


def nn(a, b):
    return jnp.dot(a, b, preferred_element_type=F32)


def layer_kernel(
    q_hbm, k_hbm, v_hbm, og_hbm, gain_ref, w_hbm,
    dq_hbm, dk_hbm, dv_hbm, wg_hbm, gg_ref,
    q, k, v, og, wall, scores_t, q_t, att, up, p, n_t, dkp, dvp, dq_o, dk_o, dv_o, wg_o,
    kvs, s0s, s0r, s1s, s1r, s2s, s2r, fin, st, zb, gflat, col,
    sib_out, sib_in, part, ra, pb_buf, rb,
    load_sem, out_sem, ag_send, ag_recv, ag_sib, sc_send, sc_recv, z_send, z_recv,
    rs_send, rs_recv, rsb_recv, pair_send, pair_recv,
):
    s = lax.axis_index("seq")
    z = lax.axis_index("dp")
    y, x, c = s // 8, (s // 2) % 4, s % 2
    o = 1 - c
    pa, pb = x + c * (y - x), y + c * (x - y)

    def chip(da, db):
        a, b = (pa + da) % 4, (pb + db) % 4
        return a * (1 + 3 * c) + b * (4 - 3 * c)

    def chip_o(da, db):
        a, b = (pb + da) % 4, (pa + db) % 4
        return a * (1 + 3 * o) + b * (4 - 3 * o)

    def dev(da, db):
        return (2 * chip(da, db) + c, z)

    sib = (s + 1 - 2 * c, z)

    loads = [
        pltpu.make_async_copy(src, dst, load_sem.at[i])
        for i, (src, dst) in enumerate(
            [(k_hbm, k), (v_hbm, v), (w_hbm, wall.at[s]), (q_hbm, q), (og_hbm, og)]
        )
    ]
    for load in loads:
        load.start()

    barrier = pltpu.get_barrier_semaphore()
    partners = [dev(i, 0) for i in (1, 2, 3)] + [dev(0, i) for i in (1, 2, 3)] + [sib]
    partners += [(s, (z + i) % 8) for i in range(1, 8)]
    for d in partners:
        pl.semaphore_signal(barrier, inc=1, device_id=d, device_id_type=MESH)

    def send(src, dst, ssem, rsem, d):
        pltpu.make_async_remote_copy(
            src_ref=src, dst_ref=dst, send_sem=ssem, recv_sem=rsem,
            device_id=d, device_id_type=MESH,
        ).start()

    def await_(ref, sem):
        pltpu.make_async_copy(ref, ref, sem).wait()

    def head(h):
        return pl.ds(pl.multiple_of(h * HD, HD), HD)

    def rows(h, n=HD):
        return pl.ds(pl.multiple_of(h * n, n), n)

    lane = lax.broadcasted_iota(jnp.int32, (HD, HD), 1)
    subl = lax.broadcasted_iota(jnp.int32, (HD, HD), 0)
    eye = lane == subl

    def to_rows(column):
        return jnp.sum(jnp.where(eye, column, 0.0), axis=0, keepdims=True)

    def to_column(row):
        return jnp.sum(jnp.where(eye, row, 0.0), axis=1, keepdims=True)

    def two(rows4):
        high = rows4.astype(BF).astype(F32)
        return jnp.concatenate([high, rows4 - high, jnp.zeros((8, HD), F32)], axis=0)

    def one(rows16):
        return rows16[:NH] + rows16[NH:2 * NH]

    def before(i, j, backward):
        return (i > j) if backward else (i < j)

    own_half = rows(c, HALF)

    def scan_start(n, extra):
        s0s[n, 0:HALF, :] = kvs[n, rows(o, HALF), :]
        s0s[n, HALF:, :] = extra
        send(s0s.at[n], s0r.at[n], sc_send.at[n, 0], sc_recv.at[n, 0], sib)

    def scan_ring_a(n, extra):
        await_(s0r.at[n], sc_recv.at[n, 0])
        s1s[n, 0:HALF, :] = (kvs[n, own_half, :] + s0r[n, 0:HALF, :]).astype(BF)
        s1s[n, HALF:, :] = two(one(extra + s0r[n, HALF:, :])).astype(BF)
        for i in (1, 2, 3):
            send(s1s.at[n], s1r.at[n, i - 1], sc_send.at[n, 1], sc_recv.at[n, i], dev(i, 0))

    def scan_ring_b(n, backward):
        for i in (1, 2, 3):
            await_(s1r.at[n, i - 1], sc_recv.at[n, i])
        mine = s1s[n].astype(F32)
        lower, total = jnp.zeros_like(mine), mine
        for i in (1, 2, 3):
            got = s1r[n, i - 1].astype(F32)
            flag = before((pa - i + 4) % 4, pa, backward)
            lower = lower + jnp.where(flag, got, 0.0)
            total = total + got
        first = c == 0
        low = jnp.where(first, total, lower)
        high = jnp.where(first, total, lower + mine)
        s2s[n, 0, 0:HALF, :] = low[:HALF].astype(BF)
        s2s[n, 1, 0:HALF, :] = high[:HALF].astype(BF)
        s2s[n, 0, HALF:, :] = two(one(total[HALF:])).astype(BF)
        s2s[n, 1, HALF:, :] = two(one(total[HALF:])).astype(BF)
        for i in (1, 2, 3):
            pick = before(pb, (pb + i) % 4, backward).astype(jnp.int32)
            send(s2s.at[n, pick], s2r.at[n, i - 1], sc_send.at[n, 2], sc_recv.at[n, 3 + i], dev(0, i))
        return lower[:HALF], total[HALF:]

    def scan_last(n, backward, lower, extra):
        for i in (1, 2, 3):
            await_(s2r.at[n, i - 1], sc_recv.at[n, 3 + i])
        for i in (1, 2, 3):
            got = s2r[n, i - 1].astype(F32)
            flag = jnp.logical_or(c == 1, before((pb - i + 4) % 4, pb, backward))
            lower = lower + jnp.where(flag, got[:HALF], 0.0)
            extra = extra + got[HALF:]
        far = 0 if backward else 1
        fin[n] = (lower + jnp.where(o == far, kvs[n, own_half, :], 0.0)).astype(BF)
        send(fin.at[n], st.at[n, own_half], sc_send.at[n, 3], sc_recv.at[n, 7], sib)
        st[n, own_half, :] = (lower + jnp.where(c == far, s0r[n, 0:HALF, :], 0.0)).astype(BF)
        return one(extra)

    def scan_end(n):
        await_(fin.at[n], sc_recv.at[n, 7])

    def scan_drain(n):
        await_(s0s.at[n], sc_send.at[n, 0])
        await_(s1r.at[n], sc_send.at[n, 1])
        await_(s2r.at[n], sc_send.at[n, 2])
        await_(fin.at[n], sc_send.at[n, 3])

    def z_start(n):
        for i in range(1, 8):
            slot = zb.at[n, z]
            send(slot, slot, z_send.at[n], z_recv.at[n, i - 1], (s, (z + i) % 8))

    def z_end(n):
        for i in range(1, 8):
            await_(zb.at[n, z], z_recv.at[n, i - 1])
        total = zb[n, 0]
        for i in range(1, 8):
            total = total + zb[n, i]
        return total

    def z_drain(n):
        await_(zb.at[n, pl.ds(0, 7)], z_send.at[n])

    low_rows, high_rows = pl.ds(0, HALF), pl.ds(HALF, HALF)

    def piece(da, db):
        return wall.at[2 * chip(da, db) + c]

    def piece_o(da, db):
        return wall.at[2 * chip_o(da, db) + o]

    halves = (low_rows, high_rows)

    def ag_half(ref, half, event, d):
        part_ref = ref.at[halves[half]]
        send(part_ref, part_ref, ag_send.at[0], ag_recv.at[event], d)

    def ag_wait(ref, half, event):
        await_(ref.at[halves[half]], ag_recv.at[event])

    def ag_pair(ref, i, j):
        send(ref, ref, ag_send.at[0], ag_sib.at[4 * i + j], sib)

    def ag_own():
        ref = piece(0, 0)
        ag_half(ref, 0, 0, dev(1, 0))
        ag_half(ref, 1, 3, dev(3, 0))
        ag_half(ref, 1, 1, dev(1, 0))
        ag_half(ref, 0, 2, dev(3, 0))

    def ag_own_b():
        ref = piece(0, 0)
        ag_half(ref, 0, 6, dev(0, 1))
        ag_half(ref, 1, 9, dev(0, 3))
        ag_half(ref, 1, 7, dev(0, 1))
        ag_half(ref, 0, 8, dev(0, 3))
        ag_pair(ref, 0, 0)

    def ag_both(ref, i, half):
        ag_half(ref, half, 6 + 6 * i + half, dev(0, 1))
        ag_half(ref, half, 8 + 6 * i + half, dev(0, 3))

    def ag_a_first():
        ref = piece(3, 0)
        ag_wait(ref, 0, 0)
        ag_half(ref, 0, 4, dev(1, 0))
        ag_both(ref, 1, 0)
        ref = piece(1, 0)
        ag_wait(ref, 1, 3)
        ag_half(ref, 1, 5, dev(3, 0))
        ag_both(ref, 2, 1)

    def ag_a_rest():
        ref = piece(3, 0)
        ag_wait(ref, 1, 1)
        ag_both(ref, 1, 1)
        ag_pair(ref, 1, 0)
        ref = piece(1, 0)
        ag_wait(ref, 0, 2)
        ag_both(ref, 2, 0)
        ag_pair(ref, 2, 0)

    def ag_a_far():
        ref = piece(2, 0)
        ag_wait(ref, 0, 4)
        ag_both(ref, 3, 0)
        ag_wait(ref, 1, 5)
        ag_both(ref, 3, 1)
        ag_pair(ref, 3, 0)

    def ag_b_up(i):
        ref = piece(STEPS[i], 3)
        ag_wait(ref, 0, 6 + 6 * i)
        ag_half(ref, 0, 10 + 6 * i, dev(0, 1))

    def ag_b_down(i):
        ref = piece(STEPS[i], 1)
        ag_wait(ref, 1, 9 + 6 * i)
        ag_half(ref, 1, 11 + 6 * i, dev(0, 3))

    def ag_b_rest(i):
        ref = piece(STEPS[i], 3)
        ag_wait(ref, 1, 7 + 6 * i)
        ag_pair(ref, i, 1)
        ref = piece(STEPS[i], 1)
        ag_wait(ref, 0, 8 + 6 * i)
        ag_pair(ref, i, 2)

    def ag_b_far(i):
        ref = piece(STEPS[i], 2)
        ag_wait(ref, 0, 10 + 6 * i)
        ag_wait(ref, 1, 11 + 6 * i)
        ag_pair(ref, i, 3)

    def ag_1():
        ag_a_first()
        ag_b_up(0)
        ag_b_down(0)

    def ag_2():
        ag_a_rest()
        ag_a_far()

    def ag_3():
        ag_b_rest(0)
        ag_b_up(1)
        ag_b_down(2)
        ag_b_down(1)
        ag_b_up(2)

    def ag_4():
        ag_b_far(0)
        ag_b_up(3)
        ag_b_down(3)
        ag_b_rest(1)
        ag_b_rest(2)

    def ag_5():
        ag_b_far(1)
        ag_b_far(2)
        ag_b_rest(3)
        ag_b_far(3)

    def ag_pair_end(j):
        for i in range(4):
            await_(piece_o(STEPS[i], STEPS[j]), ag_sib.at[4 * i + j])

    def ag_drain():
        await_(wall.at[pl.ds(0, 31)], ag_send.at[0])

    def upstream(j):
        mine = [2 * chip(STEPS[i], STEPS[j]) + c for i in range(4)]
        mine += [2 * chip_o(STEPS[i], STEPS[j]) + o for i in range(4)]
        grad = jnp.concatenate([og[:, head(m)] for m in mine], axis=1)
        for n in (0, HALF):
            weight = jnp.concatenate([wall[m, n:n + HALF, :] for m in mine], axis=1)
            term = nt(grad, weight)
            up[:, n:n + HALF] = term if j == 0 else up[:, n:n + HALF] + term

    def ordered(j):
        return jnp.where(j == 0, 2, jnp.where(j == 3, 0, jnp.where(j == 1, 1, 3)))

    def rs_pair_out(lo, hi):
        def pair(i, _):
            jb, h = i // 2, i % 2
            db = ordered(jb)
            m0 = 2 * chip_o(ordered(2 * h), db) + o
            m1 = 2 * chip_o(ordered(2 * h + 1), db) + o
            term = nn(n_t[...], jnp.concatenate([og[:, head(m0)], og[:, head(m1)]], axis=1))
            sib_out[2 * i] = term[:, :HD].astype(BF)
            sib_out[2 * i + 1] = term[:, HD:].astype(BF)
            slot = pl.ds(2 * i, 2)
            send(sib_out.at[slot], sib_in.at[slot], pair_send.at[0], pair_recv.at[i], sib)
            return _

        lax.fori_loop(lo, hi, pair, 0)

    def rs_send_to(src, dst, rsem, d):
        send(src, dst, rs_send.at[0], rsem, d)

    def rs_own(lo, hi):
        def group(jb, _):
            db = ordered(jb)
            for h in (0, 1):
                m0 = 2 * chip(ORDER[2 * h], db) + c
                m1 = 2 * chip(ORDER[2 * h + 1], db) + c
                term = nn(n_t[...], jnp.concatenate([og[:, head(m0)], og[:, head(m1)]], axis=1))
                i = 2 * jb + h
                await_(sib_in.at[pl.ds(2 * i, 2)], pair_recv.at[i])
                part[2 * i] = (term[:, :HD] + sib_in[2 * i].astype(F32)).astype(BF)
                part[2 * i + 1] = (term[:, HD:] + sib_in[2 * i + 1].astype(F32)).astype(BF)
                if h == 0:
                    far, near = part.at[2 * i], part.at[2 * i + 1]
                    rs_send_to(far.at[low_rows], ra.at[jb, 0], rs_recv.at[jb, 0], dev(1, 0))
                    rs_send_to(far.at[high_rows], ra.at[jb, 1], rs_recv.at[jb, 1], dev(3, 0))
                    rs_send_to(near.at[high_rows], ra.at[jb, 2], rs_recv.at[jb, 2], dev(1, 0))
                else:
                    near = part.at[2 * i]
                    rs_send_to(near.at[low_rows], ra.at[jb, 4], rs_recv.at[jb, 4], dev(3, 0))
            return _

        lax.fori_loop(lo, hi, group, 0)

    def rs_a_mid(jb):
        await_(ra.at[jb, 0], rs_recv.at[jb, 0])
        m = 4 * jb + 1
        part[m, 0:HALF, :] = (part[m, 0:HALF, :].astype(F32) + ra[jb, 0].astype(F32)).astype(BF)
        rs_send_to(part.at[m, low_rows], ra.at[jb, 3], rs_recv.at[jb, 3], dev(1, 0))
        await_(ra.at[jb, 1], rs_recv.at[jb, 1])
        m = 4 * jb + 2
        part[m, HALF:, :] = (part[m, HALF:, :].astype(F32) + ra[jb, 1].astype(F32)).astype(BF)
        rs_send_to(part.at[m, high_rows], ra.at[jb, 5], rs_recv.at[jb, 5], dev(3, 0))

    def rs_a_end(jb):
        for i in (2, 3, 4, 5):
            await_(ra.at[jb, i], rs_recv.at[jb, i])
        m = 4 * jb + 3
        top = part[m, 0:HALF, :].astype(F32) + ra[jb, 3].astype(F32) + ra[jb, 4].astype(F32)
        low = part[m, HALF:, :].astype(F32) + ra[jb, 2].astype(F32) + ra[jb, 5].astype(F32)
        if jb == 3:
            wg_o[0:HALF, :] = top
            wg_o[HALF:, :] = low
            return
        pb_buf[jb, 0:HALF, :] = top.astype(BF)
        pb_buf[jb, HALF:, :] = low.astype(BF)
        ref = pb_buf.at[jb]
        if jb == 0:
            rs_send_to(ref.at[low_rows], rb.at[0], rsb_recv.at[0], dev(0, 1))
            rs_send_to(ref.at[high_rows], rb.at[1], rsb_recv.at[1], dev(0, 3))
        elif jb == 1:
            rs_send_to(ref.at[high_rows], rb.at[2], rsb_recv.at[2], dev(0, 1))
        else:
            rs_send_to(ref.at[low_rows], rb.at[4], rsb_recv.at[4], dev(0, 3))

    def rs_b_mid():
        await_(rb.at[0], rsb_recv.at[0])
        pb_buf[1, 0:HALF, :] = (pb_buf[1, 0:HALF, :].astype(F32) + rb[0].astype(F32)).astype(BF)
        rs_send_to(pb_buf.at[1, low_rows], rb.at[3], rsb_recv.at[3], dev(0, 1))
        await_(rb.at[1], rsb_recv.at[1])
        pb_buf[2, HALF:, :] = (pb_buf[2, HALF:, :].astype(F32) + rb[1].astype(F32)).astype(BF)
        rs_send_to(pb_buf.at[2, high_rows], rb.at[5], rsb_recv.at[5], dev(0, 3))

    def rs_b_end():
        for i in (2, 3, 4, 5):
            await_(rb.at[i], rsb_recv.at[i])
        wg_o[0:HALF, :] = wg_o[0:HALF, :] + rb[3].astype(F32) + rb[4].astype(F32)
        wg_o[HALF:, :] = wg_o[HALF:, :] + rb[2].astype(F32) + rb[5].astype(F32)

    def rs_drain():
        await_(sib_in.at[pl.ds(0, 15)], rs_send.at[0])
        await_(sib_out, pair_send.at[0])

    tri_r = lax.broadcasted_iota(jnp.int32, (HALF, HALF), 0)
    tri_u = lax.broadcasted_iota(jnp.int32, (HALF, HALF), 1)

    def lower_part(a, b):
        return jnp.where(tri_u <= tri_r, nt(a, b), 0.0).astype(BF)

    def upper_part(a, b):
        return jnp.where(tri_u >= tri_r, nt(a, b), 0.0).astype(BF)

    top, bot = slice(0, HALF), slice(HALF, TOK)

    def forward_head(h):
        l = head(h)
        q0, q1, k0, k1 = q[top, l], q[bot, l], k[top, l], k[bot, l]
        att[top, l] = nn(lower_part(q0, k0), v[top, l])
        both = jnp.concatenate([nt(q1, k0).astype(BF), lower_part(q1, k1)], axis=1)
        att[bot, l] = nn(both, v[:, l])
        scores_t[h, top, top] = upper_part(k0, q0)
        scores_t[h, top, bot] = nt(k0, q1).astype(BF)
        scores_t[h, bot, bot] = upper_part(k1, q1)

    def back_head(h):
        l = head(h)
        p0, p1, v0, v1 = p[top, l], p[bot, l], v[top, l], v[bot, l]
        state = st[0, rows(h), :]
        dq_o[top, l] = (nn(lower_part(p0, v0), k[top, l]) + nt(p0, state)).astype(BF)
        both = jnp.concatenate([nt(p1, v0).astype(BF), lower_part(p1, v1)], axis=1)
        dq_o[bot, l] = (nn(both, k[:, l]) + nt(p1, state)).astype(BF)
        both = jnp.concatenate([upper_part(v0, p0), nt(v0, p1).astype(BF)], axis=1)
        dkp[top, l] = nn(both, q[:, l])
        dkp[bot, l] = nn(upper_part(v1, p1), q[bot, l])
        dvp[top, l] = nn(scores_t[h, top, :], p[:, l])
        dvp[bot, l] = nn(scores_t[h, bot, bot], p1)

    def loop(lo, hi, f):
        def step(h, _):
            f(h)
            return _

        lax.fori_loop(lo, hi, step, 0)

    lane4 = lax.broadcasted_iota(jnp.int32, (NH, HD), 1)
    placed = jnp.zeros((NH, HD), F32)
    for j in range(4):
        placed = placed + jnp.where(lane4 == 4 * s + j, gain_ref[:, j:j + 1].astype(F32), 0.0)
    placed = jnp.concatenate([placed, jnp.zeros((16 - NH, HD), F32)], axis=0)
    loads[2].wait()
    pl.semaphore_wait(barrier, 14)
    ag_own()
    loads[0].wait()
    loads[1].wait()
    for h in range(NH):
        l = slice(h * HD, (h + 1) * HD)
        kvs[0, l, :] = tn(k[:, l], v[:, l])
    scan_start(0, placed)
    loads[3].wait()
    scan_ring_a(0, placed)
    ag_own_b()
    loop(0, 1, forward_head)
    ag_1()
    loop(1, 3, forward_head)
    lower, extra = scan_ring_b(0, False)
    ag_2()
    loop(3, 4, forward_head)
    gains = scan_last(0, False, lower, extra)
    ag_3()
    for h in range(NH):
        gflat[0:1, h * HD:(h + 1) * HD] = gains[h:h + 1]
        q_t[h] = q[:, h * HD:(h + 1) * HD].T
    ag_4()
    scan_end(0)

    for h in range(NH):
        l = slice(h * HD, (h + 1) * HD)
        a = att[:, l] + nn(q[:, l], st[0, l, :])
        att[:, l] = a
        col[0] = a * a if h == 0 else col[0] + a * a
    for t in range(4):
        l = slice(t * 128, (t + 1) * 128)
        zb[0, z, t:t + 1, :] = to_rows(jnp.sum(col[0, l, :], axis=1, keepdims=True))
    z_start(0)
    loads[4].wait()
    ag_pair_end(0)
    upstream(0)
    ag_5()
    ag_pair_end(1)
    upstream(1)
    ag_pair_end(2)
    upstream(2)
    ag_pair_end(3)
    upstream(3)

    def inner_block(t, _):
        r = rows(t, 128)
        total = jnp.zeros((HD, HD), F32)
        for h in range(NH):
            l = slice(h * HD, (h + 1) * HD)
            total = total + up[r, l] * gflat[0:1, l] * att[r, l]
        zb[1, z, pl.ds(t, 1), :] = to_rows(jnp.sum(total, axis=1, keepdims=True))
        return _

    lax.fori_loop(0, 4, inner_block, 0)
    z_start(1)
    squares = z_end(0)
    inv = lax.rsqrt(squares / D + EPSILON)
    for t in range(4):
        col[0, t * 128:(t + 1) * 128, :] = jnp.broadcast_to(to_column(inv[t:t + 1]), (HD, HD))

    def normed_block(t, _):
        r = rows(t, 128)
        for h in range(NH):
            l = slice(h * HD, (h + 1) * HD)
            normed = att[r, l] * col[0, r, :] * gflat[0:1, l]
            n_t[l, head(t)] = normed.astype(BF).T
        return _

    lax.fori_loop(0, 4, normed_block, 0)
    rs_pair_out(0, 4)
    rs_own(0, 1)
    rs_pair_out(4, 6)
    rs_own(1, 2)
    rs_pair_out(6, 8)
    rs_own(2, 4)
    inner = z_end(1)
    for t in range(4):
        pair = inv[t:t + 1] * inv[t:t + 1] * inv[t:t + 1] * inner[t:t + 1] / D
        col[1, t * 128:(t + 1) * 128, :] = jnp.broadcast_to(to_column(pair), (HD, HD))

    def grad_block(t, sums):
        r = rows(t, 128)
        out = []
        for h in range(NH):
            l = slice(h * HD, (h + 1) * HD)
            a, u, i = att[r, l], up[r, l], col[0, r, :]
            p[r, l] = (i * u * gflat[0:1, l] - a * col[1, r, :]).astype(BF)
            out.append(sums[h] + jnp.sum(u * a * i, axis=0, keepdims=True))
        return tuple(out)

    sums = lax.fori_loop(0, 4, grad_block, (jnp.zeros((1, HD), F32),) * NH)
    gain_part = jnp.concatenate(list(sums), axis=0)

    for h in range(NH):
        l = slice(h * HD, (h + 1) * HD)
        kvs[1, l, :] = nn(q_t[h], p[:, l])
    scan_start(1, two(gain_part))
    loop(0, 1, back_head)
    scan_ring_a(1, two(gain_part))
    rs_a_mid(0)
    rs_a_mid(1)
    rs_a_mid(2)
    rs_a_mid(3)
    loop(1, 2, back_head)
    lower, extra = scan_ring_b(1, True)
    rs_a_end(0)
    rs_a_end(1)
    loop(2, 3, back_head)
    gain_total = scan_last(1, True, lower, extra)
    rs_a_end(2)
    rs_b_mid()
    loop(3, 4, back_head)
    dq_copy = pltpu.make_async_copy(dq_o, dq_hbm, out_sem.at[0])
    dq_copy.start()
    for j in range(4):
        gg_ref[:, j:j + 1] = jnp.sum(
            jnp.where(lane4 == 4 * s + j, gain_total, 0.0), axis=1, keepdims=True
        )
    scan_end(1)
    for h in range(NH):
        l = slice(h * HD, (h + 1) * HD)
        dk_o[:, l] = (dkp[:, l] + nt(v[:, l], st[1, l, :])).astype(BF)
        dv_o[:, l] = (dvp[:, l] + nn(k[:, l], st[1, l, :])).astype(BF)
    dk_copy = pltpu.make_async_copy(dk_o, dk_hbm, out_sem.at[1])
    dv_copy = pltpu.make_async_copy(dv_o, dv_hbm, out_sem.at[2])
    dk_copy.start()
    dv_copy.start()
    ag_drain()
    scan_drain(0)
    z_drain(0)
    z_drain(1)
    rs_a_end(3)
    rs_b_end()
    wg_copy = pltpu.make_async_copy(wg_o, wg_hbm, out_sem.at[3])
    wg_copy.start()
    rs_drain()
    scan_drain(1)
    for copy in (dq_copy, dk_copy, dv_copy, wg_copy):
        copy.wait()


def copy_kernel(a, b, d, e, f, a_o, b_o, d_o, e_o, f_o, sem):
    copies = [
        pltpu.make_async_copy(src, dst, sem.at[i])
        for i, (src, dst) in enumerate([(a, a_o), (b, b_o), (d, d_o), (e, e_o), (f, f_o)])
    ]
    for copy in copies:
        copy.start()
    for copy in copies:
        copy.wait()


def body(queries, keys, values, out_grad, gain, out_weight):
    any_space = pl.BlockSpec(memory_space=pl.ANY)
    hbm = pl.BlockSpec(memory_space=pltpu.HBM)
    vmem = pl.BlockSpec(memory_space=pltpu.VMEM)
    sem = pltpu.SemaphoreType.DMA
    outs = (
        jax.ShapeDtypeStruct((TOK, WID), BF),
        jax.ShapeDtypeStruct((TOK, WID), BF),
        jax.ShapeDtypeStruct((TOK, WID), BF),
        jax.ShapeDtypeStruct((WID, HD), F32),
        jax.ShapeDtypeStruct((NH, 4), F32),
    )
    wide = lambda dt: pltpu.VMEM((TOK, WID), dt)
    results = pl.pallas_call(
        layer_kernel,
        out_shape=outs,
        in_specs=[hbm, hbm, hbm, hbm, vmem, hbm],
        out_specs=(any_space, any_space, any_space, any_space, vmem),
        scratch_shapes=[
            wide(BF), wide(BF), wide(BF),
            pltpu.VMEM((TOK, D), BF),
            pltpu.VMEM((32, WID, HD), BF),
            pltpu.VMEM((NH, TOK, TOK), BF),
            pltpu.VMEM((NH, HD, TOK), BF),
            wide(F32), wide(F32), wide(BF), wide(BF), wide(F32), wide(F32),
            wide(BF), wide(BF), wide(BF),
            pltpu.VMEM((WID, HD), F32),
            pltpu.VMEM((2, WID, HD), F32),
            pltpu.VMEM((2, HALF + 16, HD), F32),
            pltpu.VMEM((2, HALF + 16, HD), F32),
            pltpu.VMEM((2, HALF + 16, HD), BF),
            pltpu.VMEM((2, 3, HALF + 16, HD), BF),
            pltpu.VMEM((2, 2, HALF + 16, HD), BF),
            pltpu.VMEM((2, 3, HALF + 16, HD), BF),
            pltpu.VMEM((2, HALF, HD), BF),
            pltpu.VMEM((2, WID, HD), BF),
            pltpu.VMEM((2, 8, 4, HD), F32),
            pltpu.VMEM((1, WID), F32),
            pltpu.VMEM((2, TOK, HD), F32),
            pltpu.VMEM((16, WID, HD), BF),
            pltpu.VMEM((16, WID, HD), BF),
            pltpu.VMEM((16, WID, HD), BF),
            pltpu.VMEM((4, 6, HALF, HD), BF),
            pltpu.VMEM((3, WID, HD), BF),
            pltpu.VMEM((6, HALF, HD), BF),
            sem((5,)), sem((4,)), sem((1,)), sem((30,)), sem((16,)),
            sem((2, 4)), sem((2, 8)), sem((2,)), sem((2, 7)),
            sem((1,)), sem((4, 6)), sem((6,)), sem((1,)), sem((8,)),
        ],
        compiler_params=pltpu.CompilerParams(
            collective_id=0, has_side_effects=True, vmem_limit_bytes=52 * 2**20
        ),
        cost_estimate=pl.CostEstimate(
            flops=6_400_000_000, bytes_accessed=8_000_000, transcendentals=512
        ),
        name="layer",
    )(queries, keys, values, out_grad, gain, out_weight)
    return pl.pallas_call(
        copy_kernel,
        out_shape=outs,
        in_specs=[any_space] * 5,
        out_specs=(hbm,) * 5,
        scratch_shapes=[sem((5,))],
        compiler_params=pltpu.CompilerParams(vmem_limit_bytes=2**20),
        name="results",
    )(*results)


def solution(mesh):
    return jax.shard_map(
        body,
        mesh=mesh,
        in_specs=(
            P("seq", "dp"),
            P("seq", "dp"),
            P("seq", "dp"),
            P("seq", None),
            P("dp", "seq"),
            P("dp", "seq"),
        ),
        out_specs=(P("seq", "dp"), P("seq", "dp"), P("seq", "dp"), P("dp", "seq"), P("dp", "seq")),
        check_vma=False,
    )
```

```python
import jax
import jax.numpy as jnp
from jax import lax
from jax.experimental import pallas as pl
from jax.experimental.pallas import tpu as pltpu
from jax.sharding import PartitionSpec as P

HD = 128
TOK = 512
WID = 512
NH = 4
D = 4096
EPSILON = 1e-06
HALF = 256
BF = jnp.bfloat16
F32 = jnp.float32
MESH = pl.DeviceIdType.MESH
STEPS = (0, 3, 1, 2)
ORDER = (2, 1, 3, 0)


def nt(a, b):
    return lax.dot_general(a, b, (((1,), (1,)), ((), ())), preferred_element_type=F32)


def tn(a, b):
    return lax.dot_general(a, b, (((0,), (0,)), ((), ())), preferred_element_type=F32)


def nn(a, b):
    return jnp.dot(a, b, preferred_element_type=F32)


def layer_kernel(
    q_hbm, k_hbm, v_hbm, og_hbm, gain_ref, w_hbm,
    dq_hbm, dk_hbm, dv_hbm, wg_hbm, gg_ref,
    q, k, v, og, wall, scores_t, q_t, att, up, p, n_t, dkp, dvp, dq_o, dk_o, dv_o, wg_o,
    kvs, s0s, s0r, s1s, s1r, s2s, s2r, fin, st, zb, gflat, col,
    sib_out, sib_in, part, ra, pb_buf, rb,
    load_sem, out_sem, ag_send, ag_recv, ag_sib, sc_send, sc_recv, z_send, z_recv,
    rs_send, rs_recv, rsb_recv, pair_send, pair_recv,
):
    s = lax.axis_index("seq")
    z = lax.axis_index("dp")
    y, x, c = s // 8, (s // 2) % 4, s % 2
    o = 1 - c
    pa, pb = x + c * (y - x), y + c * (x - y)

    def chip(da, db):
        a, b = (pa + da) % 4, (pb + db) % 4
        return a * (1 + 3 * c) + b * (4 - 3 * c)

    def chip_o(da, db):
        a, b = (pb + da) % 4, (pa + db) % 4
        return a * (1 + 3 * o) + b * (4 - 3 * o)

    def dev(da, db):
        return (2 * chip(da, db) + c, z)

    sib = (s + 1 - 2 * c, z)

    loads = [
        pltpu.make_async_copy(src, dst, load_sem.at[i])
        for i, (src, dst) in enumerate(
            [(k_hbm, k), (v_hbm, v), (w_hbm, wall.at[s]), (q_hbm, q), (og_hbm, og)]
        )
    ]
    for load in loads:
        load.start()

    barrier = pltpu.get_barrier_semaphore()
    partners = [dev(i, 0) for i in (1, 2, 3)] + [dev(0, i) for i in (1, 2, 3)] + [sib]
    partners += [(s, (z + i) % 8) for i in range(1, 8)]
    for d in partners:
        pl.semaphore_signal(barrier, inc=1, device_id=d, device_id_type=MESH)

    def send(src, dst, ssem, rsem, d):
        pltpu.make_async_remote_copy(
            src_ref=src, dst_ref=dst, send_sem=ssem, recv_sem=rsem,
            device_id=d, device_id_type=MESH,
        ).start()

    def await_(ref, sem):
        pltpu.make_async_copy(ref, ref, sem).wait()

    def head(h):
        return pl.ds(pl.multiple_of(h * HD, HD), HD)

    def rows(h, n=HD):
        return pl.ds(pl.multiple_of(h * n, n), n)

    lane = lax.broadcasted_iota(jnp.int32, (HD, HD), 1)
    subl = lax.broadcasted_iota(jnp.int32, (HD, HD), 0)
    eye = lane == subl

    def to_rows(column):
        return jnp.sum(jnp.where(eye, column, 0.0), axis=0, keepdims=True)

    def to_column(row):
        return jnp.sum(jnp.where(eye, row, 0.0), axis=1, keepdims=True)

    def two(rows4):
        high = rows4.astype(BF).astype(F32)
        return jnp.concatenate([high, rows4 - high, jnp.zeros((8, HD), F32)], axis=0)

    def one(rows16):
        return rows16[:NH] + rows16[NH:2 * NH]

    def before(i, j, backward):
        return (i > j) if backward else (i < j)

    own_half = rows(c, HALF)

    def scan_start(n, extra):
        s0s[n, 0:HALF, :] = kvs[n, rows(o, HALF), :]
        s0s[n, HALF:, :] = extra
        send(s0s.at[n], s0r.at[n], sc_send.at[n, 0], sc_recv.at[n, 0], sib)

    def scan_ring_a(n, extra):
        await_(s0r.at[n], sc_recv.at[n, 0])
        s1s[n, 0:HALF, :] = (kvs[n, own_half, :] + s0r[n, 0:HALF, :]).astype(BF)
        s1s[n, HALF:, :] = two(one(extra + s0r[n, HALF:, :])).astype(BF)
        for i in (2, 1, 3):
            send(s1s.at[n], s1r.at[n, i - 1], sc_send.at[n, 1], sc_recv.at[n, i], dev(i, 0))

    def scan_ring_b(n, backward):
        for i in (1, 2, 3):
            await_(s1r.at[n, i - 1], sc_recv.at[n, i])
        mine = s1s[n].astype(F32)
        lower, total = jnp.zeros_like(mine), mine
        for i in (1, 2, 3):
            got = s1r[n, i - 1].astype(F32)
            flag = before((pa - i + 4) % 4, pa, backward)
            lower = lower + jnp.where(flag, got, 0.0)
            total = total + got
        first = c == 0
        low = jnp.where(first, total, lower)
        high = jnp.where(first, total, lower + mine)
        s2s[n, 0, 0:HALF, :] = low[:HALF].astype(BF)
        s2s[n, 1, 0:HALF, :] = high[:HALF].astype(BF)
        s2s[n, 0, HALF:, :] = two(one(total[HALF:])).astype(BF)
        s2s[n, 1, HALF:, :] = two(one(total[HALF:])).astype(BF)
        for i in (2, 1, 3):
            pick = before(pb, (pb + i) % 4, backward).astype(jnp.int32)
            send(s2s.at[n, pick], s2r.at[n, i - 1], sc_send.at[n, 2], sc_recv.at[n, 3 + i], dev(0, i))
        return lower[:HALF], total[HALF:]

    def scan_last(n, backward, lower, extra):
        for i in (1, 2, 3):
            await_(s2r.at[n, i - 1], sc_recv.at[n, 3 + i])
        for i in (1, 2, 3):
            got = s2r[n, i - 1].astype(F32)
            flag = jnp.logical_or(c == 1, before((pb - i + 4) % 4, pb, backward))
            lower = lower + jnp.where(flag, got[:HALF], 0.0)
            extra = extra + got[HALF:]
        far = 0 if backward else 1
        fin[n] = (lower + jnp.where(o == far, kvs[n, own_half, :], 0.0)).astype(BF)
        send(fin.at[n], st.at[n, own_half], sc_send.at[n, 3], sc_recv.at[n, 7], sib)
        st[n, own_half, :] = (lower + jnp.where(c == far, s0r[n, 0:HALF, :], 0.0)).astype(BF)
        return one(extra)

    def scan_end(n):
        await_(fin.at[n], sc_recv.at[n, 7])

    def scan_drain(n):
        await_(s0s.at[n], sc_send.at[n, 0])
        await_(s1r.at[n], sc_send.at[n, 1])
        await_(s2r.at[n], sc_send.at[n, 2])
        await_(fin.at[n], sc_send.at[n, 3])

    def z_start(n):
        for i in (4, 3, 5, 2, 6, 1, 7):
            slot = zb.at[n, z]
            send(slot, slot, z_send.at[n], z_recv.at[n, i - 1], (s, (z + i) % 8))

    def z_end(n):
        for i in range(1, 8):
            await_(zb.at[n, z], z_recv.at[n, i - 1])
        total = zb[n, 0]
        for i in range(1, 8):
            total = total + zb[n, i]
        return total

    def z_drain(n):
        await_(zb.at[n, pl.ds(0, 7)], z_send.at[n])

    low_rows, high_rows = pl.ds(0, HALF), pl.ds(HALF, HALF)

    def piece(da, db):
        return wall.at[2 * chip(da, db) + c]

    def piece_o(da, db):
        return wall.at[2 * chip_o(da, db) + o]

    halves = (low_rows, high_rows)

    def ag_half(ref, half, event, d):
        part_ref = ref.at[halves[half]]
        send(part_ref, part_ref, ag_send.at[0], ag_recv.at[event], d)

    def ag_wait(ref, half, event):
        await_(ref.at[halves[half]], ag_recv.at[event])

    def ag_pair(ref, i, j):
        send(ref, ref, ag_send.at[0], ag_sib.at[4 * i + j], sib)

    def ag_own():
        ref = piece(0, 0)
        ag_half(ref, 0, 0, dev(1, 0))
        ag_half(ref, 1, 3, dev(3, 0))
        ag_half(ref, 1, 1, dev(1, 0))
        ag_half(ref, 0, 2, dev(3, 0))

    def ag_own_b():
        ref = piece(0, 0)
        ag_half(ref, 0, 6, dev(0, 1))
        ag_half(ref, 1, 9, dev(0, 3))
        ag_half(ref, 1, 7, dev(0, 1))
        ag_half(ref, 0, 8, dev(0, 3))
        ag_pair(ref, 0, 0)

    def ag_both(ref, i, half):
        ag_half(ref, half, 6 + 6 * i + half, dev(0, 1))
        ag_half(ref, half, 8 + 6 * i + half, dev(0, 3))

    def ag_a_first():
        ref = piece(3, 0)
        ag_wait(ref, 0, 0)
        ag_half(ref, 0, 4, dev(1, 0))
        ag_both(ref, 1, 0)
        ref = piece(1, 0)
        ag_wait(ref, 1, 3)
        ag_half(ref, 1, 5, dev(3, 0))
        ag_both(ref, 2, 1)

    def ag_a_rest():
        ref = piece(3, 0)
        ag_wait(ref, 1, 1)
        ag_both(ref, 1, 1)
        ag_pair(ref, 1, 0)
        ref = piece(1, 0)
        ag_wait(ref, 0, 2)
        ag_both(ref, 2, 0)
        ag_pair(ref, 2, 0)

    def ag_a_far():
        ref = piece(2, 0)
        ag_wait(ref, 0, 4)
        ag_both(ref, 3, 0)
        ag_wait(ref, 1, 5)
        ag_both(ref, 3, 1)
        ag_pair(ref, 3, 0)

    def ag_b_up(i):
        ref = piece(STEPS[i], 3)
        ag_wait(ref, 0, 6 + 6 * i)
        ag_half(ref, 0, 10 + 6 * i, dev(0, 1))

    def ag_b_down(i):
        ref = piece(STEPS[i], 1)
        ag_wait(ref, 1, 9 + 6 * i)
        ag_half(ref, 1, 11 + 6 * i, dev(0, 3))

    def ag_b_rest(i):
        ref = piece(STEPS[i], 3)
        ag_wait(ref, 1, 7 + 6 * i)
        ag_pair(ref, i, 1)
        ref = piece(STEPS[i], 1)
        ag_wait(ref, 0, 8 + 6 * i)
        ag_pair(ref, i, 2)

    def ag_b_far(i):
        ref = piece(STEPS[i], 2)
        ag_wait(ref, 0, 10 + 6 * i)
        ag_wait(ref, 1, 11 + 6 * i)
        ag_pair(ref, i, 3)

    def ag_1():
        ag_a_first()
        ag_b_up(0)
        ag_b_down(0)

    def ag_2():
        ag_a_rest()
        ag_a_far()

    def ag_3():
        ag_b_rest(0)
        ag_b_up(1)
        ag_b_down(2)
        ag_b_down(1)
        ag_b_up(2)

    def ag_4():
        ag_b_far(0)
        ag_b_up(3)
        ag_b_down(3)
        ag_b_rest(1)
        ag_b_rest(2)

    def ag_5():
        ag_b_far(1)
        ag_b_far(2)
        ag_b_rest(3)
        ag_b_far(3)

    def ag_pair_end(j):
        for i in range(4):
            await_(piece_o(STEPS[i], STEPS[j]), ag_sib.at[4 * i + j])

    def ag_drain():
        await_(wall.at[pl.ds(0, 31)], ag_send.at[0])

    def upstream(j):
        mine = [2 * chip(STEPS[i], STEPS[j]) + c for i in range(4)]
        mine += [2 * chip_o(STEPS[i], STEPS[j]) + o for i in range(4)]
        grad = jnp.concatenate([og[:, head(m)] for m in mine], axis=1)
        for n in (0, HALF):
            weight = jnp.concatenate([wall[m, n:n + HALF, :] for m in mine], axis=1)
            term = nt(grad, weight)
            up[:, n:n + HALF] = term if j == 0 else up[:, n:n + HALF] + term

    def ordered(j):
        return jnp.where(j == 0, 2, jnp.where(j == 3, 0, jnp.where(j == 1, 1, 3)))

    def rs_pair_out(lo, hi):
        def pair(i, _):
            jb, h = i // 2, i % 2
            db = ordered(jb)
            m0 = 2 * chip_o(ordered(2 * h), db) + o
            m1 = 2 * chip_o(ordered(2 * h + 1), db) + o
            term = nn(n_t[...], jnp.concatenate([og[:, head(m0)], og[:, head(m1)]], axis=1))
            sib_out[2 * i] = term[:, :HD].astype(BF)
            sib_out[2 * i + 1] = term[:, HD:].astype(BF)
            slot = pl.ds(2 * i, 2)
            send(sib_out.at[slot], sib_in.at[slot], pair_send.at[0], pair_recv.at[i], sib)
            return _

        lax.fori_loop(lo, hi, pair, 0)

    def rs_send_to(src, dst, rsem, d):
        send(src, dst, rs_send.at[0], rsem, d)

    def rs_own(lo, hi):
        def group(jb, _):
            db = ordered(jb)
            for h in (0, 1):
                m0 = 2 * chip(ORDER[2 * h], db) + c
                m1 = 2 * chip(ORDER[2 * h + 1], db) + c
                term = nn(n_t[...], jnp.concatenate([og[:, head(m0)], og[:, head(m1)]], axis=1))
                i = 2 * jb + h
                await_(sib_in.at[pl.ds(2 * i, 2)], pair_recv.at[i])
                part[2 * i] = (term[:, :HD] + sib_in[2 * i].astype(F32)).astype(BF)
                part[2 * i + 1] = (term[:, HD:] + sib_in[2 * i + 1].astype(F32)).astype(BF)
                if h == 0:
                    far, near = part.at[2 * i], part.at[2 * i + 1]
                    rs_send_to(far.at[low_rows], ra.at[jb, 0], rs_recv.at[jb, 0], dev(1, 0))
                    rs_send_to(far.at[high_rows], ra.at[jb, 1], rs_recv.at[jb, 1], dev(3, 0))
                    rs_send_to(near.at[high_rows], ra.at[jb, 2], rs_recv.at[jb, 2], dev(1, 0))
                else:
                    near = part.at[2 * i]
                    rs_send_to(near.at[low_rows], ra.at[jb, 4], rs_recv.at[jb, 4], dev(3, 0))
            return _

        lax.fori_loop(lo, hi, group, 0)

    def rs_a_mid(jb):
        await_(ra.at[jb, 0], rs_recv.at[jb, 0])
        m = 4 * jb + 1
        part[m, 0:HALF, :] = (part[m, 0:HALF, :].astype(F32) + ra[jb, 0].astype(F32)).astype(BF)
        rs_send_to(part.at[m, low_rows], ra.at[jb, 3], rs_recv.at[jb, 3], dev(1, 0))
        await_(ra.at[jb, 1], rs_recv.at[jb, 1])
        m = 4 * jb + 2
        part[m, HALF:, :] = (part[m, HALF:, :].astype(F32) + ra[jb, 1].astype(F32)).astype(BF)
        rs_send_to(part.at[m, high_rows], ra.at[jb, 5], rs_recv.at[jb, 5], dev(3, 0))

    def rs_a_end(jb):
        for i in (2, 3, 4, 5):
            await_(ra.at[jb, i], rs_recv.at[jb, i])
        m = 4 * jb + 3
        top = part[m, 0:HALF, :].astype(F32) + ra[jb, 3].astype(F32) + ra[jb, 4].astype(F32)
        low = part[m, HALF:, :].astype(F32) + ra[jb, 2].astype(F32) + ra[jb, 5].astype(F32)
        if jb == 3:
            wg_o[0:HALF, :] = top
            wg_o[HALF:, :] = low
            return
        pb_buf[jb, 0:HALF, :] = top.astype(BF)
        pb_buf[jb, HALF:, :] = low.astype(BF)
        ref = pb_buf.at[jb]
        if jb == 0:
            rs_send_to(ref.at[low_rows], rb.at[0], rsb_recv.at[0], dev(0, 1))
            rs_send_to(ref.at[high_rows], rb.at[1], rsb_recv.at[1], dev(0, 3))
        elif jb == 1:
            rs_send_to(ref.at[high_rows], rb.at[2], rsb_recv.at[2], dev(0, 1))
        else:
            rs_send_to(ref.at[low_rows], rb.at[4], rsb_recv.at[4], dev(0, 3))

    def rs_b_mid():
        await_(rb.at[0], rsb_recv.at[0])
        pb_buf[1, 0:HALF, :] = (pb_buf[1, 0:HALF, :].astype(F32) + rb[0].astype(F32)).astype(BF)
        rs_send_to(pb_buf.at[1, low_rows], rb.at[3], rsb_recv.at[3], dev(0, 1))
        await_(rb.at[1], rsb_recv.at[1])
        pb_buf[2, HALF:, :] = (pb_buf[2, HALF:, :].astype(F32) + rb[1].astype(F32)).astype(BF)
        rs_send_to(pb_buf.at[2, high_rows], rb.at[5], rsb_recv.at[5], dev(0, 3))

    def rs_b_end():
        for i in (2, 3, 4, 5):
            await_(rb.at[i], rsb_recv.at[i])
        wg_o[0:HALF, :] = wg_o[0:HALF, :] + rb[3].astype(F32) + rb[4].astype(F32)
        wg_o[HALF:, :] = wg_o[HALF:, :] + rb[2].astype(F32) + rb[5].astype(F32)

    def rs_drain():
        await_(sib_in.at[pl.ds(0, 15)], rs_send.at[0])
        await_(sib_out, pair_send.at[0])

    tri_r = lax.broadcasted_iota(jnp.int32, (HALF, HALF), 0)
    tri_u = lax.broadcasted_iota(jnp.int32, (HALF, HALF), 1)

    def lower_part(a, b):
        return jnp.where(tri_u <= tri_r, nt(a, b), 0.0).astype(BF)

    def upper_part(a, b):
        return jnp.where(tri_u >= tri_r, nt(a, b), 0.0).astype(BF)

    top, bot = slice(0, HALF), slice(HALF, TOK)

    def forward_head(h):
        l = head(h)
        q0, q1, k0, k1 = q[top, l], q[bot, l], k[top, l], k[bot, l]
        att[top, l] = nn(lower_part(q0, k0), v[top, l])
        both = jnp.concatenate([nt(q1, k0).astype(BF), lower_part(q1, k1)], axis=1)
        att[bot, l] = nn(both, v[:, l])
        scores_t[h, top, top] = upper_part(k0, q0)
        scores_t[h, top, bot] = nt(k0, q1).astype(BF)
        scores_t[h, bot, bot] = upper_part(k1, q1)

    def back_head(h):
        l = head(h)
        p0, p1, v0, v1 = p[top, l], p[bot, l], v[top, l], v[bot, l]
        state = st[0, rows(h), :]
        dq_o[top, l] = (nn(lower_part(p0, v0), k[top, l]) + nt(p0, state)).astype(BF)
        both = jnp.concatenate([nt(p1, v0).astype(BF), lower_part(p1, v1)], axis=1)
        dq_o[bot, l] = (nn(both, k[:, l]) + nt(p1, state)).astype(BF)
        both = jnp.concatenate([upper_part(v0, p0), nt(v0, p1).astype(BF)], axis=1)
        dkp[top, l] = nn(both, q[:, l])
        dkp[bot, l] = nn(upper_part(v1, p1), q[bot, l])
        dvp[top, l] = nn(scores_t[h, top, :], p[:, l])
        dvp[bot, l] = nn(scores_t[h, bot, bot], p1)

    def loop(lo, hi, f):
        def step(h, _):
            f(h)
            return _

        lax.fori_loop(lo, hi, step, 0)

    lane4 = lax.broadcasted_iota(jnp.int32, (NH, HD), 1)
    placed = jnp.zeros((NH, HD), F32)
    for j in range(4):
        placed = placed + jnp.where(lane4 == 4 * s + j, gain_ref[:, j:j + 1].astype(F32), 0.0)
    placed = jnp.concatenate([placed, jnp.zeros((16 - NH, HD), F32)], axis=0)
    loads[2].wait()
    pl.semaphore_wait(barrier, 14)
    ag_own()
    loads[0].wait()
    loads[1].wait()
    for i in (2 * o, 2 * o + 1):
        kvs[0, rows(i), :] = tn(k[:, head(i)], v[:, head(i)])
    scan_start(0, placed)
    for i in (2 * c, 2 * c + 1):
        kvs[0, rows(i), :] = tn(k[:, head(i)], v[:, head(i)])
    loads[3].wait()
    scan_ring_a(0, placed)
    ag_own_b()
    loop(0, 1, forward_head)
    ag_1()
    loop(1, 3, forward_head)
    lower, extra = scan_ring_b(0, False)
    ag_2()
    loop(3, 4, forward_head)
    gains = scan_last(0, False, lower, extra)
    ag_3()
    for h in range(NH):
        gflat[0:1, h * HD:(h + 1) * HD] = gains[h:h + 1]
        q_t[h] = q[:, h * HD:(h + 1) * HD].T
    ag_4()
    scan_end(0)

    for h in range(NH):
        l = slice(h * HD, (h + 1) * HD)
        a = att[:, l] + nn(q[:, l], st[0, l, :])
        att[:, l] = a
        col[0] = a * a if h == 0 else col[0] + a * a
    for t in range(4):
        l = slice(t * 128, (t + 1) * 128)
        zb[0, z, t:t + 1, :] = to_rows(jnp.sum(col[0, l, :], axis=1, keepdims=True))
    z_start(0)
    loads[4].wait()
    ag_pair_end(0)
    upstream(0)
    ag_5()
    ag_pair_end(1)
    upstream(1)
    ag_pair_end(2)
    upstream(2)
    ag_pair_end(3)
    upstream(3)

    def inner_block(t, _):
        r = rows(t, 128)
        total = jnp.zeros((HD, HD), F32)
        for h in range(NH):
            l = slice(h * HD, (h + 1) * HD)
            total = total + up[r, l] * gflat[0:1, l] * att[r, l]
        zb[1, z, pl.ds(t, 1), :] = to_rows(jnp.sum(total, axis=1, keepdims=True))
        return _

    lax.fori_loop(0, 4, inner_block, 0)
    z_start(1)
    squares = z_end(0)
    inv = lax.rsqrt(squares / D + EPSILON)
    for t in range(4):
        col[0, t * 128:(t + 1) * 128, :] = jnp.broadcast_to(to_column(inv[t:t + 1]), (HD, HD))

    def normed_block(t, _):
        r = rows(t, 128)
        for h in range(NH):
            l = slice(h * HD, (h + 1) * HD)
            normed = att[r, l] * col[0, r, :] * gflat[0:1, l]
            n_t[l, head(t)] = normed.astype(BF).T
        return _

    lax.fori_loop(0, 4, normed_block, 0)
    rs_pair_out(0, 4)
    rs_own(0, 1)
    rs_pair_out(4, 6)
    rs_own(1, 2)
    rs_pair_out(6, 8)
    rs_own(2, 4)
    inner = z_end(1)
    for t in range(4):
        pair = inv[t:t + 1] * inv[t:t + 1] * inv[t:t + 1] * inner[t:t + 1] / D
        col[1, t * 128:(t + 1) * 128, :] = jnp.broadcast_to(to_column(pair), (HD, HD))

    def grad_block(t, sums):
        r = rows(t, 128)
        out = []
        for h in range(NH):
            l = slice(h * HD, (h + 1) * HD)
            a, u, i = att[r, l], up[r, l], col[0, r, :]
            p[r, l] = (i * u * gflat[0:1, l] - a * col[1, r, :]).astype(BF)
            out.append(sums[h] + jnp.sum(u * a * i, axis=0, keepdims=True))
        return tuple(out)

    sums = lax.fori_loop(0, 4, grad_block, (jnp.zeros((1, HD), F32),) * NH)
    gain_part = jnp.concatenate(list(sums), axis=0)

    for i in (2 * o, 2 * o + 1):
        kvs[1, rows(i), :] = nn(q_t[i], p[:, head(i)])
    scan_start(1, two(gain_part))
    for i in (2 * c, 2 * c + 1):
        kvs[1, rows(i), :] = nn(q_t[i], p[:, head(i)])
    loop(0, 1, back_head)
    scan_ring_a(1, two(gain_part))
    rs_a_mid(0)
    rs_a_mid(1)
    rs_a_mid(2)
    rs_a_mid(3)
    loop(1, 2, back_head)
    lower, extra = scan_ring_b(1, True)
    rs_a_end(0)
    rs_a_end(1)
    loop(2, 3, back_head)
    gain_total = scan_last(1, True, lower, extra)
    rs_a_end(2)
    rs_b_mid()
    loop(3, 4, back_head)
    dq_copy = pltpu.make_async_copy(dq_o, dq_hbm, out_sem.at[0])
    dq_copy.start()
    for j in range(4):
        gg_ref[:, j:j + 1] = jnp.sum(
            jnp.where(lane4 == 4 * s + j, gain_total, 0.0), axis=1, keepdims=True
        )
    scan_end(1)
    for h in range(NH):
        l = slice(h * HD, (h + 1) * HD)
        dk_o[:, l] = (dkp[:, l] + nt(v[:, l], st[1, l, :])).astype(BF)
        dv_o[:, l] = (dvp[:, l] + nn(k[:, l], st[1, l, :])).astype(BF)
    dk_copy = pltpu.make_async_copy(dk_o, dk_hbm, out_sem.at[1])
    dv_copy = pltpu.make_async_copy(dv_o, dv_hbm, out_sem.at[2])
    dk_copy.start()
    dv_copy.start()
    ag_drain()
    scan_drain(0)
    z_drain(0)
    z_drain(1)
    rs_a_end(3)
    rs_b_end()
    wg_copy = pltpu.make_async_copy(wg_o, wg_hbm, out_sem.at[3])
    wg_copy.start()
    rs_drain()
    scan_drain(1)
    for copy in (dq_copy, dk_copy, dv_copy, wg_copy):
        copy.wait()


def copy_kernel(a, b, d, e, f, a_o, b_o, d_o, e_o, f_o, sem):
    copies = [
        pltpu.make_async_copy(src, dst, sem.at[i])
        for i, (src, dst) in enumerate([(a, a_o), (b, b_o), (d, d_o), (e, e_o), (f, f_o)])
    ]
    for copy in copies:
        copy.start()
    for copy in copies:
        copy.wait()


def body(queries, keys, values, out_grad, gain, out_weight):
    any_space = pl.BlockSpec(memory_space=pl.ANY)
    hbm = pl.BlockSpec(memory_space=pltpu.HBM)
    vmem = pl.BlockSpec(memory_space=pltpu.VMEM)
    sem = pltpu.SemaphoreType.DMA
    outs = (
        jax.ShapeDtypeStruct((TOK, WID), BF),
        jax.ShapeDtypeStruct((TOK, WID), BF),
        jax.ShapeDtypeStruct((TOK, WID), BF),
        jax.ShapeDtypeStruct((WID, HD), F32),
        jax.ShapeDtypeStruct((NH, 4), F32),
    )
    wide = lambda dt: pltpu.VMEM((TOK, WID), dt)
    results = pl.pallas_call(
        layer_kernel,
        out_shape=outs,
        in_specs=[hbm, hbm, hbm, hbm, vmem, hbm],
        out_specs=(any_space, any_space, any_space, any_space, vmem),
        scratch_shapes=[
            wide(BF), wide(BF), wide(BF),
            pltpu.VMEM((TOK, D), BF),
            pltpu.VMEM((32, WID, HD), BF),
            pltpu.VMEM((NH, TOK, TOK), BF),
            pltpu.VMEM((NH, HD, TOK), BF),
            wide(F32), wide(F32), wide(BF), wide(BF), wide(F32), wide(F32),
            wide(BF), wide(BF), wide(BF),
            pltpu.VMEM((WID, HD), F32),
            pltpu.VMEM((2, WID, HD), F32),
            pltpu.VMEM((2, HALF + 16, HD), F32),
            pltpu.VMEM((2, HALF + 16, HD), F32),
            pltpu.VMEM((2, HALF + 16, HD), BF),
            pltpu.VMEM((2, 3, HALF + 16, HD), BF),
            pltpu.VMEM((2, 2, HALF + 16, HD), BF),
            pltpu.VMEM((2, 3, HALF + 16, HD), BF),
            pltpu.VMEM((2, HALF, HD), BF),
            pltpu.VMEM((2, WID, HD), BF),
            pltpu.VMEM((2, 8, 4, HD), F32),
            pltpu.VMEM((1, WID), F32),
            pltpu.VMEM((2, TOK, HD), F32),
            pltpu.VMEM((16, WID, HD), BF),
            pltpu.VMEM((16, WID, HD), BF),
            pltpu.VMEM((16, WID, HD), BF),
            pltpu.VMEM((4, 6, HALF, HD), BF),
            pltpu.VMEM((3, WID, HD), BF),
            pltpu.VMEM((6, HALF, HD), BF),
            sem((5,)), sem((4,)), sem((1,)), sem((30,)), sem((16,)),
            sem((2, 4)), sem((2, 8)), sem((2,)), sem((2, 7)),
            sem((1,)), sem((4, 6)), sem((6,)), sem((1,)), sem((8,)),
        ],
        compiler_params=pltpu.CompilerParams(
            collective_id=0, has_side_effects=True, vmem_limit_bytes=52 * 2**20
        ),
        cost_estimate=pl.CostEstimate(
            flops=6_400_000_000, bytes_accessed=8_000_000, transcendentals=512
        ),
        name="layer",
    )(queries, keys, values, out_grad, gain, out_weight)
    return pl.pallas_call(
        copy_kernel,
        out_shape=outs,
        in_specs=[any_space] * 5,
        out_specs=(hbm,) * 5,
        scratch_shapes=[sem((5,))],
        compiler_params=pltpu.CompilerParams(vmem_limit_bytes=2**20),
        name="results",
    )(*results)


def solution(mesh):
    return jax.shard_map(
        body,
        mesh=mesh,
        in_specs=(
            P("seq", "dp"),
            P("seq", "dp"),
            P("seq", "dp"),
            P("seq", None),
            P("dp", "seq"),
            P("dp", "seq"),
        ),
        out_specs=(P("seq", "dp"), P("seq", "dp"), P("seq", "dp"), P("dp", "seq"), P("dp", "seq")),
        check_vma=False,
    )
```

```python
import jax
import jax.numpy as jnp
from jax import lax
from jax.experimental import pallas as pl
from jax.experimental.pallas import tpu as pltpu
from jax.sharding import PartitionSpec as P

HD = 128
TOK = 512
WID = 512
NH = 4
D = 4096
EPSILON = 1e-06
HALF = 256
BF = jnp.bfloat16
F32 = jnp.float32
MESH = pl.DeviceIdType.MESH
STEPS = (0, 3, 1, 2)
ORDER = (2, 1, 3, 0)


def nt(a, b):
    return lax.dot_general(a, b, (((1,), (1,)), ((), ())), preferred_element_type=F32)


def tn(a, b):
    return lax.dot_general(a, b, (((0,), (0,)), ((), ())), preferred_element_type=F32)


def nn(a, b):
    return jnp.dot(a, b, preferred_element_type=F32)


def layer_kernel(
    q_hbm, k_hbm, v_hbm, og_hbm, gain_ref, w_hbm,
    dq_hbm, dk_hbm, dv_hbm, wg_hbm, gg_ref,
    q, k, v, og, wall, scores_t, q_t, att, up, p, n_t, dkp, dvp, dq_o, dk_o, dv_o, wg_o,
    kvs, s0s, s0r, s1s, s1r, s2s, s2r, fin, st, zb, gflat, col,
    sib_out, sib_in, part, ra, pb_buf, rb,
    load_sem, out_sem, ag_send, ag_recv, ag_sib, sc_send, sc_recv, z_send, z_recv,
    rs_send, rs_recv, rsb_recv, pair_send, pair_recv,
):
    s = lax.axis_index("seq")
    z = lax.axis_index("dp")
    y, x, c = s // 8, (s // 2) % 4, s % 2
    o = 1 - c
    pa, pb = x + c * (y - x), y + c * (x - y)

    def chip(da, db):
        a, b = (pa + da) % 4, (pb + db) % 4
        return a * (1 + 3 * c) + b * (4 - 3 * c)

    def chip_o(da, db):
        a, b = (pb + da) % 4, (pa + db) % 4
        return a * (1 + 3 * o) + b * (4 - 3 * o)

    def dev(da, db):
        return (2 * chip(da, db) + c, z)

    sib = (s + 1 - 2 * c, z)

    loads = [
        pltpu.make_async_copy(src, dst, load_sem.at[i])
        for i, (src, dst) in enumerate(
            [(k_hbm, k), (v_hbm, v), (w_hbm, wall.at[s]), (q_hbm, q), (og_hbm, og)]
        )
    ]
    for load in loads:
        load.start()

    barrier = pltpu.get_barrier_semaphore()
    partners = [dev(i, 0) for i in (1, 2, 3)] + [dev(0, i) for i in (1, 2, 3)] + [sib]
    partners += [(s, (z + i) % 8) for i in range(1, 8)]
    for d in partners:
        pl.semaphore_signal(barrier, inc=1, device_id=d, device_id_type=MESH)

    def send(src, dst, ssem, rsem, d):
        pltpu.make_async_remote_copy(
            src_ref=src, dst_ref=dst, send_sem=ssem, recv_sem=rsem,
            device_id=d, device_id_type=MESH,
        ).start()

    def await_(ref, sem):
        pltpu.make_async_copy(ref, ref, sem).wait()

    def head(h):
        return pl.ds(pl.multiple_of(h * HD, HD), HD)

    def rows(h, n=HD):
        return pl.ds(pl.multiple_of(h * n, n), n)

    lane = lax.broadcasted_iota(jnp.int32, (HD, HD), 1)
    subl = lax.broadcasted_iota(jnp.int32, (HD, HD), 0)
    eye = lane == subl

    def to_rows(column):
        return jnp.sum(jnp.where(eye, column, 0.0), axis=0, keepdims=True)

    def to_column(row):
        return jnp.sum(jnp.where(eye, row, 0.0), axis=1, keepdims=True)

    def two(rows4):
        high = rows4.astype(BF).astype(F32)
        return jnp.concatenate([high, rows4 - high, jnp.zeros((8, HD), F32)], axis=0)

    def one(rows16):
        return rows16[:NH] + rows16[NH:2 * NH]

    def before(i, j, backward):
        return (i > j) if backward else (i < j)

    own_half = rows(c, HALF)

    def scan_start(n, extra):
        s0s[n, 0:HALF, :] = kvs[n, rows(o, HALF), :]
        s0s[n, HALF:, :] = extra
        send(s0s.at[n], s0r.at[n], sc_send.at[n, 0], sc_recv.at[n, 0], sib)

    def scan_ring_a(n, extra):
        await_(s0r.at[n], sc_recv.at[n, 0])
        s1s[n, 0:HALF, :] = (kvs[n, own_half, :] + s0r[n, 0:HALF, :]).astype(BF)
        s1s[n, HALF:, :] = two(one(extra + s0r[n, HALF:, :])).astype(BF)
        for i in (2, 1, 3):
            send(s1s.at[n], s1r.at[n, i - 1], sc_send.at[n, 1], sc_recv.at[n, i], dev(i, 0))

    def scan_ring_b(n, backward):
        for i in (1, 2, 3):
            await_(s1r.at[n, i - 1], sc_recv.at[n, i])
        mine = s1s[n].astype(F32)
        lower, total = jnp.zeros_like(mine), mine
        for i in (1, 2, 3):
            got = s1r[n, i - 1].astype(F32)
            flag = before((pa - i + 4) % 4, pa, backward)
            lower = lower + jnp.where(flag, got, 0.0)
            total = total + got
        first = c == 0
        low = jnp.where(first, total, lower)
        high = jnp.where(first, total, lower + mine)
        s2s[n, 0, 0:HALF, :] = low[:HALF].astype(BF)
        s2s[n, 1, 0:HALF, :] = high[:HALF].astype(BF)
        s2s[n, 0, HALF:, :] = two(one(total[HALF:])).astype(BF)
        s2s[n, 1, HALF:, :] = two(one(total[HALF:])).astype(BF)
        for i in (2, 1, 3):
            pick = before(pb, (pb + i) % 4, backward).astype(jnp.int32)
            send(s2s.at[n, pick], s2r.at[n, i - 1], sc_send.at[n, 2], sc_recv.at[n, 3 + i], dev(0, i))
        return lower[:HALF], total[HALF:]

    def scan_last(n, backward, lower, extra):
        for i in (1, 2, 3):
            await_(s2r.at[n, i - 1], sc_recv.at[n, 3 + i])
        for i in (1, 2, 3):
            got = s2r[n, i - 1].astype(F32)
            flag = jnp.logical_or(c == 1, before((pb - i + 4) % 4, pb, backward))
            lower = lower + jnp.where(flag, got[:HALF], 0.0)
            extra = extra + got[HALF:]
        far = 0 if backward else 1
        fin[n] = (lower + jnp.where(o == far, kvs[n, own_half, :], 0.0)).astype(BF)
        send(fin.at[n], st.at[n, own_half], sc_send.at[n, 3], sc_recv.at[n, 7], sib)
        st[n, own_half, :] = (lower + jnp.where(c == far, s0r[n, 0:HALF, :], 0.0)).astype(BF)
        return one(extra)

    def scan_end(n):
        await_(fin.at[n], sc_recv.at[n, 7])

    def scan_drain(n):
        await_(s0s.at[n], sc_send.at[n, 0])
        await_(s1r.at[n], sc_send.at[n, 1])
        await_(s2r.at[n], sc_send.at[n, 2])
        await_(fin.at[n], sc_send.at[n, 3])

    def z_start(n):
        for i in (4, 3, 5, 2, 6, 1, 7):
            slot = zb.at[n, z]
            send(slot, slot, z_send.at[n], z_recv.at[n, i - 1], (s, (z + i) % 8))

    def z_end(n):
        for i in range(1, 8):
            await_(zb.at[n, z], z_recv.at[n, i - 1])
        total = zb[n, 0]
        for i in range(1, 8):
            total = total + zb[n, i]
        return total

    def z_drain(n):
        await_(zb.at[n, pl.ds(0, 7)], z_send.at[n])

    low_rows, high_rows = pl.ds(0, HALF), pl.ds(HALF, HALF)

    def piece(da, db):
        return wall.at[2 * chip(da, db) + c]

    def piece_o(da, db):
        return wall.at[2 * chip_o(da, db) + o]

    halves = (low_rows, high_rows)

    def ag_half(ref, half, event, d):
        part_ref = ref.at[halves[half]]
        send(part_ref, part_ref, ag_send.at[0], ag_recv.at[event], d)

    def ag_wait(ref, half, event):
        await_(ref.at[halves[half]], ag_recv.at[event])

    def ag_pair(ref, i, j):
        send(ref, ref, ag_send.at[0], ag_sib.at[4 * i + j], sib)

    def ag_own():
        ref = piece(0, 0)
        ag_half(ref, 0, 0, dev(1, 0))
        ag_half(ref, 1, 3, dev(3, 0))
        ag_half(ref, 1, 1, dev(1, 0))
        ag_half(ref, 0, 2, dev(3, 0))

    def ag_own_b():
        ref = piece(0, 0)
        ag_half(ref, 0, 6, dev(0, 1))
        ag_half(ref, 1, 9, dev(0, 3))
        ag_half(ref, 1, 7, dev(0, 1))
        ag_half(ref, 0, 8, dev(0, 3))
        ag_pair(ref, 0, 0)

    def ag_both(ref, i, half):
        ag_half(ref, half, 6 + 6 * i + half, dev(0, 1))
        ag_half(ref, half, 8 + 6 * i + half, dev(0, 3))

    def ag_a_first():
        ref = piece(3, 0)
        ag_wait(ref, 0, 0)
        ag_half(ref, 0, 4, dev(1, 0))
        ag_both(ref, 1, 0)
        ref = piece(1, 0)
        ag_wait(ref, 1, 3)
        ag_half(ref, 1, 5, dev(3, 0))
        ag_both(ref, 2, 1)

    def ag_a_rest():
        ref = piece(3, 0)
        ag_wait(ref, 1, 1)
        ag_both(ref, 1, 1)
        ag_pair(ref, 1, 0)
        ref = piece(1, 0)
        ag_wait(ref, 0, 2)
        ag_both(ref, 2, 0)
        ag_pair(ref, 2, 0)

    def ag_a_far():
        ref = piece(2, 0)
        ag_wait(ref, 0, 4)
        ag_both(ref, 3, 0)
        ag_wait(ref, 1, 5)
        ag_both(ref, 3, 1)
        ag_pair(ref, 3, 0)

    def ag_b_up(i):
        ref = piece(STEPS[i], 3)
        ag_wait(ref, 0, 6 + 6 * i)
        ag_half(ref, 0, 10 + 6 * i, dev(0, 1))

    def ag_b_down(i):
        ref = piece(STEPS[i], 1)
        ag_wait(ref, 1, 9 + 6 * i)
        ag_half(ref, 1, 11 + 6 * i, dev(0, 3))

    def ag_b_rest(i):
        ref = piece(STEPS[i], 3)
        ag_wait(ref, 1, 7 + 6 * i)
        ag_pair(ref, i, 1)
        ref = piece(STEPS[i], 1)
        ag_wait(ref, 0, 8 + 6 * i)
        ag_pair(ref, i, 2)

    def ag_b_far(i):
        ref = piece(STEPS[i], 2)
        ag_wait(ref, 0, 10 + 6 * i)
        ag_wait(ref, 1, 11 + 6 * i)
        ag_pair(ref, i, 3)

    def ag_1():
        ag_a_first()
        ag_b_up(0)
        ag_b_down(0)

    def ag_2():
        ag_a_rest()
        ag_a_far()

    def ag_3():
        ag_b_rest(0)
        ag_b_up(1)
        ag_b_down(2)
        ag_b_down(1)
        ag_b_up(2)

    def ag_4():
        ag_b_far(0)
        ag_b_up(3)
        ag_b_down(3)
        ag_b_rest(1)
        ag_b_rest(2)

    def ag_5():
        ag_b_far(1)
        ag_b_far(2)
        ag_b_rest(3)
        ag_b_far(3)

    def ag_pair_end(j):
        for i in range(4):
            await_(piece_o(STEPS[i], STEPS[j]), ag_sib.at[4 * i + j])

    def ag_drain():
        await_(wall.at[pl.ds(0, 31)], ag_send.at[0])

    def upstream(j):
        mine = [2 * chip(STEPS[i], STEPS[j]) + c for i in range(4)]
        mine += [2 * chip_o(STEPS[i], STEPS[j]) + o for i in range(4)]
        grad = jnp.concatenate([og[:, head(m)] for m in mine], axis=1)
        for n in (0, HALF):
            weight = jnp.concatenate([wall[m, n:n + HALF, :] for m in mine], axis=1)
            term = nt(grad, weight)
            up[:, n:n + HALF] = term if j == 0 else up[:, n:n + HALF] + term

    def ordered(j):
        return jnp.where(j == 0, 2, jnp.where(j == 3, 0, jnp.where(j == 1, 1, 3)))

    def rs_pair_out(lo, hi):
        def pair(i, _):
            jb, h = i // 2, i % 2
            db = ordered(jb)
            m0 = 2 * chip_o(ordered(2 * h), db) + o
            m1 = 2 * chip_o(ordered(2 * h + 1), db) + o
            term = nn(n_t[...], jnp.concatenate([og[:, head(m0)], og[:, head(m1)]], axis=1))
            sib_out[2 * i] = term[:, :HD].astype(BF)
            sib_out[2 * i + 1] = term[:, HD:].astype(BF)
            slot = pl.ds(2 * i, 2)
            send(sib_out.at[slot], sib_in.at[slot], pair_send.at[0], pair_recv.at[i], sib)
            return _

        lax.fori_loop(lo, hi, pair, 0)

    def rs_send_to(src, dst, rsem, d):
        send(src, dst, rs_send.at[0], rsem, d)

    def rs_own(lo, hi):
        def group(jb, _):
            db = ordered(jb)
            for h in (0, 1):
                m0 = 2 * chip(ORDER[2 * h], db) + c
                m1 = 2 * chip(ORDER[2 * h + 1], db) + c
                term = nn(n_t[...], jnp.concatenate([og[:, head(m0)], og[:, head(m1)]], axis=1))
                i = 2 * jb + h
                await_(sib_in.at[pl.ds(2 * i, 2)], pair_recv.at[i])
                part[2 * i] = (term[:, :HD] + sib_in[2 * i].astype(F32)).astype(BF)
                part[2 * i + 1] = (term[:, HD:] + sib_in[2 * i + 1].astype(F32)).astype(BF)
                if h == 0:
                    far, near = part.at[2 * i], part.at[2 * i + 1]
                    rs_send_to(far.at[low_rows], ra.at[jb, 0], rs_recv.at[jb, 0], dev(1, 0))
                    rs_send_to(far.at[high_rows], ra.at[jb, 1], rs_recv.at[jb, 1], dev(3, 0))
                    rs_send_to(near.at[high_rows], ra.at[jb, 2], rs_recv.at[jb, 2], dev(1, 0))
                else:
                    near = part.at[2 * i]
                    rs_send_to(near.at[low_rows], ra.at[jb, 4], rs_recv.at[jb, 4], dev(3, 0))
            return _

        lax.fori_loop(lo, hi, group, 0)

    def rs_a_mid(jb):
        await_(ra.at[jb, 0], rs_recv.at[jb, 0])
        m = 4 * jb + 1
        part[m, 0:HALF, :] = (part[m, 0:HALF, :].astype(F32) + ra[jb, 0].astype(F32)).astype(BF)
        rs_send_to(part.at[m, low_rows], ra.at[jb, 3], rs_recv.at[jb, 3], dev(1, 0))
        await_(ra.at[jb, 1], rs_recv.at[jb, 1])
        m = 4 * jb + 2
        part[m, HALF:, :] = (part[m, HALF:, :].astype(F32) + ra[jb, 1].astype(F32)).astype(BF)
        rs_send_to(part.at[m, high_rows], ra.at[jb, 5], rs_recv.at[jb, 5], dev(3, 0))

    def rs_a_end(jb):
        for i in (2, 3, 4, 5):
            await_(ra.at[jb, i], rs_recv.at[jb, i])
        m = 4 * jb + 3
        top = part[m, 0:HALF, :].astype(F32) + ra[jb, 3].astype(F32) + ra[jb, 4].astype(F32)
        low = part[m, HALF:, :].astype(F32) + ra[jb, 2].astype(F32) + ra[jb, 5].astype(F32)
        if jb == 3:
            wg_o[0:HALF, :] = top
            wg_o[HALF:, :] = low
            return
        pb_buf[jb, 0:HALF, :] = top.astype(BF)
        pb_buf[jb, HALF:, :] = low.astype(BF)
        ref = pb_buf.at[jb]
        if jb == 0:
            rs_send_to(ref.at[low_rows], rb.at[0], rsb_recv.at[0], dev(0, 1))
            rs_send_to(ref.at[high_rows], rb.at[1], rsb_recv.at[1], dev(0, 3))
        elif jb == 1:
            rs_send_to(ref.at[high_rows], rb.at[2], rsb_recv.at[2], dev(0, 1))
        else:
            rs_send_to(ref.at[low_rows], rb.at[4], rsb_recv.at[4], dev(0, 3))

    def rs_b_mid():
        await_(rb.at[0], rsb_recv.at[0])
        pb_buf[1, 0:HALF, :] = (pb_buf[1, 0:HALF, :].astype(F32) + rb[0].astype(F32)).astype(BF)
        rs_send_to(pb_buf.at[1, low_rows], rb.at[3], rsb_recv.at[3], dev(0, 1))
        await_(rb.at[1], rsb_recv.at[1])
        pb_buf[2, HALF:, :] = (pb_buf[2, HALF:, :].astype(F32) + rb[1].astype(F32)).astype(BF)
        rs_send_to(pb_buf.at[2, high_rows], rb.at[5], rsb_recv.at[5], dev(0, 3))

    def rs_b_end():
        for i in (2, 3, 4, 5):
            await_(rb.at[i], rsb_recv.at[i])
        wg_o[0:HALF, :] = wg_o[0:HALF, :] + rb[3].astype(F32) + rb[4].astype(F32)
        wg_o[HALF:, :] = wg_o[HALF:, :] + rb[2].astype(F32) + rb[5].astype(F32)

    def rs_drain():
        await_(sib_in.at[pl.ds(0, 15)], rs_send.at[0])
        await_(sib_out, pair_send.at[0])

    tri_r = lax.broadcasted_iota(jnp.int32, (HALF, HALF), 0)
    tri_u = lax.broadcasted_iota(jnp.int32, (HALF, HALF), 1)

    def lower_part(a, b):
        return jnp.where(tri_u <= tri_r, nt(a, b), 0.0).astype(BF)

    def upper_part(a, b):
        return jnp.where(tri_u >= tri_r, nt(a, b), 0.0).astype(BF)

    top, bot = slice(0, HALF), slice(HALF, TOK)

    def forward_head(h):
        l = head(h)
        q0, q1, k0, k1 = q[top, l], q[bot, l], k[top, l], k[bot, l]
        att[top, l] = nn(lower_part(q0, k0), v[top, l])
        both = jnp.concatenate([nt(q1, k0).astype(BF), lower_part(q1, k1)], axis=1)
        att[bot, l] = nn(both, v[:, l])
        scores_t[h, top, top] = upper_part(k0, q0)
        scores_t[h, top, bot] = nt(k0, q1).astype(BF)
        scores_t[h, bot, bot] = upper_part(k1, q1)

    def back_head(h):
        l = head(h)
        p0, p1, v0, v1 = p[top, l], p[bot, l], v[top, l], v[bot, l]
        state = st[0, rows(h), :]
        dq_o[top, l] = (nn(lower_part(p0, v0), k[top, l]) + nt(p0, state)).astype(BF)
        both = jnp.concatenate([nt(p1, v0).astype(BF), lower_part(p1, v1)], axis=1)
        dq_o[bot, l] = (nn(both, k[:, l]) + nt(p1, state)).astype(BF)
        both = jnp.concatenate([upper_part(v0, p0), nt(v0, p1).astype(BF)], axis=1)
        dkp[top, l] = nn(both, q[:, l])
        dkp[bot, l] = nn(upper_part(v1, p1), q[bot, l])
        dvp[top, l] = nn(scores_t[h, top, :], p[:, l])
        dvp[bot, l] = nn(scores_t[h, bot, bot], p1)

    def loop(lo, hi, f):
        def step(h, _):
            f(h)
            return _

        lax.fori_loop(lo, hi, step, 0)

    lane4 = lax.broadcasted_iota(jnp.int32, (NH, HD), 1)
    placed = jnp.zeros((NH, HD), F32)
    for j in range(4):
        placed = placed + jnp.where(lane4 == 4 * s + j, gain_ref[:, j:j + 1].astype(F32), 0.0)
    placed = jnp.concatenate([placed, jnp.zeros((16 - NH, HD), F32)], axis=0)
    loads[2].wait()
    pl.semaphore_wait(barrier, 14)
    ag_own()
    loads[0].wait()
    loads[1].wait()
    for i in (2 * o, 2 * o + 1):
        kvs[0, rows(i), :] = tn(k[:, head(i)], v[:, head(i)])
    scan_start(0, placed)
    for i in (2 * c, 2 * c + 1):
        kvs[0, rows(i), :] = tn(k[:, head(i)], v[:, head(i)])
    loads[3].wait()
    scan_ring_a(0, placed)
    ag_own_b()
    loop(0, 1, forward_head)
    ag_1()
    loop(1, 3, forward_head)
    lower, extra = scan_ring_b(0, False)
    ag_2()
    loop(3, 4, forward_head)
    gains = scan_last(0, False, lower, extra)
    ag_3()
    for h in range(NH):
        gflat[0:1, h * HD:(h + 1) * HD] = gains[h:h + 1]
        q_t[h] = q[:, h * HD:(h + 1) * HD].T
    ag_4()
    scan_end(0)

    for h in range(NH):
        l = slice(h * HD, (h + 1) * HD)
        a = att[:, l] + nn(q[:, l], st[0, l, :])
        att[:, l] = a
        col[0] = a * a if h == 0 else col[0] + a * a
    for t in range(4):
        l = slice(t * 128, (t + 1) * 128)
        zb[0, z, t:t + 1, :] = to_rows(jnp.sum(col[0, l, :], axis=1, keepdims=True))
    z_start(0)
    loads[4].wait()
    ag_pair_end(0)
    upstream(0)
    ag_5()
    ag_pair_end(1)
    upstream(1)
    ag_pair_end(2)
    upstream(2)
    ag_pair_end(3)
    upstream(3)

    def inner_block(t, _):
        r = rows(t, 128)
        total = jnp.zeros((HD, HD), F32)
        for h in range(NH):
            l = slice(h * HD, (h + 1) * HD)
            total = total + up[r, l] * gflat[0:1, l] * att[r, l]
        zb[1, z, pl.ds(t, 1), :] = to_rows(jnp.sum(total, axis=1, keepdims=True))
        return _

    lax.fori_loop(0, 4, inner_block, 0)
    z_start(1)
    squares = z_end(0)
    inv = lax.rsqrt(squares / D + EPSILON)
    for t in range(4):
        col[0, t * 128:(t + 1) * 128, :] = jnp.broadcast_to(to_column(inv[t:t + 1]), (HD, HD))

    def normed_block(t, _):
        r = rows(t, 128)
        for h in range(NH):
            l = slice(h * HD, (h + 1) * HD)
            normed = att[r, l] * col[0, r, :] * gflat[0:1, l]
            n_t[l, head(t)] = normed.astype(BF).T
        return _

    lax.fori_loop(0, 4, normed_block, 0)
    rs_pair_out(0, 4)
    rs_own(0, 1)
    rs_pair_out(4, 6)
    rs_own(1, 2)
    rs_pair_out(6, 8)
    rs_own(2, 4)
    inner = z_end(1)
    for t in range(4):
        pair = inv[t:t + 1] * inv[t:t + 1] * inv[t:t + 1] * inner[t:t + 1] / D
        col[1, t * 128:(t + 1) * 128, :] = jnp.broadcast_to(to_column(pair), (HD, HD))

    def grad_block(t, sums):
        r = rows(t, 128)
        out = []
        for h in range(NH):
            l = slice(h * HD, (h + 1) * HD)
            a, u, i = att[r, l], up[r, l], col[0, r, :]
            p[r, l] = (i * u * gflat[0:1, l] - a * col[1, r, :]).astype(BF)
            out.append(sums[h] + jnp.sum(u * a * i, axis=0, keepdims=True))
        return tuple(out)

    sums = lax.fori_loop(0, 4, grad_block, (jnp.zeros((1, HD), F32),) * NH)
    gain_part = jnp.concatenate(list(sums), axis=0)

    for i in (2 * o, 2 * o + 1):
        kvs[1, rows(i), :] = nn(q_t[i], p[:, head(i)])
    scan_start(1, two(gain_part))
    for i in (2 * c, 2 * c + 1):
        kvs[1, rows(i), :] = nn(q_t[i], p[:, head(i)])
    loop(0, 1, back_head)
    scan_ring_a(1, two(gain_part))
    rs_a_mid(0)
    rs_a_mid(1)
    rs_a_mid(2)
    rs_a_mid(3)
    loop(1, 2, back_head)
    lower, extra = scan_ring_b(1, True)
    rs_a_end(0)
    rs_a_end(1)
    loop(2, 3, back_head)
    gain_total = scan_last(1, True, lower, extra)
    rs_a_end(2)
    rs_b_mid()
    loop(3, 4, back_head)
    dq_copy = pltpu.make_async_copy(dq_o, dq_hbm, out_sem.at[0])
    dq_copy.start()
    for j in range(4):
        gg_ref[:, j:j + 1] = jnp.sum(
            jnp.where(lane4 == 4 * s + j, gain_total, 0.0), axis=1, keepdims=True
        )
    ag_drain()
    scan_drain(0)
    z_drain(0)
    z_drain(1)
    scan_end(1)
    for h in range(NH):
        l = slice(h * HD, (h + 1) * HD)
        dk_o[:, l] = (dkp[:, l] + nt(v[:, l], st[1, l, :])).astype(BF)
    dk_copy = pltpu.make_async_copy(dk_o, dk_hbm, out_sem.at[1])
    dk_copy.start()
    for h in range(NH):
        l = slice(h * HD, (h + 1) * HD)
        dv_o[:, l] = (dvp[:, l] + nn(k[:, l], st[1, l, :])).astype(BF)
    dv_copy = pltpu.make_async_copy(dv_o, dv_hbm, out_sem.at[2])
    dv_copy.start()
    rs_a_end(3)
    rs_b_end()
    wg_copy = pltpu.make_async_copy(wg_o, wg_hbm, out_sem.at[3])
    wg_copy.start()
    rs_drain()
    scan_drain(1)
    for copy in (dq_copy, dk_copy, dv_copy, wg_copy):
        copy.wait()


def copy_kernel(a, b, d, e, f, a_o, b_o, d_o, e_o, f_o, sem):
    copies = [
        pltpu.make_async_copy(src, dst, sem.at[i])
        for i, (src, dst) in enumerate([(a, a_o), (b, b_o), (d, d_o), (e, e_o), (f, f_o)])
    ]
    for copy in copies:
        copy.start()
    for copy in copies:
        copy.wait()


def body(queries, keys, values, out_grad, gain, out_weight):
    any_space = pl.BlockSpec(memory_space=pl.ANY)
    hbm = pl.BlockSpec(memory_space=pltpu.HBM)
    vmem = pl.BlockSpec(memory_space=pltpu.VMEM)
    sem = pltpu.SemaphoreType.DMA
    outs = (
        jax.ShapeDtypeStruct((TOK, WID), BF),
        jax.ShapeDtypeStruct((TOK, WID), BF),
        jax.ShapeDtypeStruct((TOK, WID), BF),
        jax.ShapeDtypeStruct((WID, HD), F32),
        jax.ShapeDtypeStruct((NH, 4), F32),
    )
    wide = lambda dt: pltpu.VMEM((TOK, WID), dt)
    results = pl.pallas_call(
        layer_kernel,
        out_shape=outs,
        in_specs=[hbm, hbm, hbm, hbm, vmem, hbm],
        out_specs=(any_space, any_space, any_space, any_space, vmem),
        scratch_shapes=[
            wide(BF), wide(BF), wide(BF),
            pltpu.VMEM((TOK, D), BF),
            pltpu.VMEM((32, WID, HD), BF),
            pltpu.VMEM((NH, TOK, TOK), BF),
            pltpu.VMEM((NH, HD, TOK), BF),
            wide(F32), wide(F32), wide(BF), wide(BF), wide(F32), wide(F32),
            wide(BF), wide(BF), wide(BF),
            pltpu.VMEM((WID, HD), F32),
            pltpu.VMEM((2, WID, HD), F32),
            pltpu.VMEM((2, HALF + 16, HD), F32),
            pltpu.VMEM((2, HALF + 16, HD), F32),
            pltpu.VMEM((2, HALF + 16, HD), BF),
            pltpu.VMEM((2, 3, HALF + 16, HD), BF),
            pltpu.VMEM((2, 2, HALF + 16, HD), BF),
            pltpu.VMEM((2, 3, HALF + 16, HD), BF),
            pltpu.VMEM((2, HALF, HD), BF),
            pltpu.VMEM((2, WID, HD), BF),
            pltpu.VMEM((2, 8, 4, HD), F32),
            pltpu.VMEM((1, WID), F32),
            pltpu.VMEM((2, TOK, HD), F32),
            pltpu.VMEM((16, WID, HD), BF),
            pltpu.VMEM((16, WID, HD), BF),
            pltpu.VMEM((16, WID, HD), BF),
            pltpu.VMEM((4, 6, HALF, HD), BF),
            pltpu.VMEM((3, WID, HD), BF),
            pltpu.VMEM((6, HALF, HD), BF),
            sem((5,)), sem((4,)), sem((1,)), sem((30,)), sem((16,)),
            sem((2, 4)), sem((2, 8)), sem((2,)), sem((2, 7)),
            sem((1,)), sem((4, 6)), sem((6,)), sem((1,)), sem((8,)),
        ],
        compiler_params=pltpu.CompilerParams(
            collective_id=0, has_side_effects=True, vmem_limit_bytes=52 * 2**20
        ),
        cost_estimate=pl.CostEstimate(
            flops=6_400_000_000, bytes_accessed=8_000_000, transcendentals=512
        ),
        name="layer",
    )(queries, keys, values, out_grad, gain, out_weight)
    return pl.pallas_call(
        copy_kernel,
        out_shape=outs,
        in_specs=[any_space] * 5,
        out_specs=(hbm,) * 5,
        scratch_shapes=[sem((5,))],
        compiler_params=pltpu.CompilerParams(vmem_limit_bytes=2**20),
        name="results",
    )(*results)


def solution(mesh):
    return jax.shard_map(
        body,
        mesh=mesh,
        in_specs=(
            P("seq", "dp"),
            P("seq", "dp"),
            P("seq", "dp"),
            P("seq", None),
            P("dp", "seq"),
            P("dp", "seq"),
        ),
        out_specs=(P("seq", "dp"), P("seq", "dp"), P("seq", "dp"), P("dp", "seq"), P("dp", "seq")),
        check_vma=False,
    )
```
